1024 devices in a mesh: row: 64 (over y, x), col: 8 (over z), split: 2 (over core).
Axes of the slice: x: 8, y: 8, z: 8, core: 2. Of those that a mesh axis runs over, the one named last changes fastest.
Arguments:
- coefficients: bfloat16 [16384, 6144], P(('row', 'col', 'split')), may hold values from -0.796875 to 0.796875
- row_weight: float32 [16384], P(('row', 'col', 'split')), may hold values from 0.1 to 1
- pattern: int32 [128, 48], replicated, may hold values 0 or 1
- aux_sizes: int32 [48], replicated, may hold values from 32 to 128
Outputs:
- response: float32 [6144, 6144], P(('row', 'split'), 'col')
The draws below stay inside these ranges and needn't reach their ends.
All inputs are finite; a program needn't handle non-finite values.
Results may differ from the reference program's by a relative error of at most 0.0015.
Values may be sent and summed in bfloat16 or wider, within the bound.
No kernel may reach another device: no remote copies, remote signals or barrier semaphores. Data moves between devices by JAX's collectives and lax.ppermute only.
A program may use at most 64 MiB of HBM per device.

```python
import math
import jax
import jax.numpy as jnp

PAIR_ROWS = 128
AUX_ATOMS = 48
AUX_PAD = 128
NA = 6144
TOTAL_ROWS = 16384
NPAIRS = 128


def draw_aux_sizes(key, part):
    key = jax.random.fold_in(key, 7)
    first, second = jax.random.split(key)
    sizes = jax.random.randint(first, (AUX_ATOMS,), AUX_PAD // 4, AUX_PAD + 1)
    where = jax.random.randint(second, (), 0, AUX_ATOMS)
    return jnp.where(jnp.arange(AUX_ATOMS) == where, AUX_PAD, sizes).astype(jnp.int32)


def plant(drawn, key, smallest, top_value):
    extent = drawn.shape
    index_at = [jax.random.randint(jax.random.fold_in(key, axis), (), 0, extent[axis]) for axis in range(len(extent))]
    drawn = drawn.at[tuple(index_at)].set(smallest)
    longest = extent.index(max(extent))
    index_at[longest] = (index_at[longest] + 1) % extent[longest]
    return drawn.at[tuple(index_at)].set(top_value)


def levels(own_key, dims, pieces, least, top_value):
    loudness = 1.0
    for dim, shards_of in pieces:
        draws = jax.random.uniform(jax.random.fold_in(jax.random.fold_in(own_key, 6), dim), (shards_of,), jnp.float32, least / len(pieces), top_value / len(pieces))
        loudness = loudness * jnp.repeat(jnp.exp(draws), dims[dim] // shards_of).reshape((-1,) + (1,) * (len(dims) - 1 - dim))
    return loudness


def noise(key, extent, scale, most, pieces=(), kind=jnp.bfloat16):
    result = scale * jax.random.normal(key, extent, jnp.float32)
    if pieces:
        result = result * levels(key, extent, pieces, -0.22, 0.18)
    return jnp.clip(result, -most, most).astype(kind)


def setup_inputs(seed: int = 0) -> dict:
    splits = jax.random.split(jax.random.key(seed), 5)
    return {
        "coefficients": noise(splits[0], (TOTAL_ROWS, NA), 0.1, 0.796875, ((0, 1024),)),
        "row_weight": jnp.clip(jnp.exp(math.log(1.0) - 2.3025851 * jax.random.uniform(splits[1], (TOTAL_ROWS,), jnp.float32) ** levels(splits[1], (TOTAL_ROWS,), ((0, 1024),), -0.2, 0.2)), 0.1, 1.0),
        "pattern": plant((jax.random.randint(splits[2], (NPAIRS, AUX_ATOMS), 0, 2) < 1).astype(jnp.int32), jax.random.fold_in(splits[2], 1), 0, 1),
        "aux_sizes": draw_aux_sizes(jax.random.fold_in(splits[4], 71), 0),
    }


def reference(coefficients, row_weight, pattern, aux_sizes):
    rows = coefficients.shape[0]
    width = AUX_ATOMS * AUX_PAD
    pat_rows = jnp.repeat(pattern, PAIR_ROWS, axis=0)
    column = jnp.arange(AUX_PAD, dtype=jnp.int32)
    col_mask = (column[None, :] < aux_sizes[:, None]).astype(jnp.int32)
    valid = (pat_rows[:, :, None] * col_mask[None, :, :]).reshape(rows, width)
    masked = coefficients * valid.astype(coefficients.dtype)
    scaled = (row_weight[:, None] * masked.astype(jnp.float32)).astype(jnp.bfloat16)
    return jnp.dot(masked.T, scaled, preferred_element_type=jnp.float32)
```

```python
import functools
import itertools

import jax
import jax.numpy as jnp
from jax import lax
from jax.experimental import pallas as pl
from jax.experimental.pallas import tpu as pltpu
from jax.sharding import Mesh, PartitionSpec as P

PAIR_ROWS = 128
AUX_PAD = 128
N = 8
AXES = ("y", "x", "z", "c")
SMEM = pl.BlockSpec(memory_space=pltpu.SMEM)
VMEM = pl.BlockSpec(memory_space=pltpu.VMEM)


def groups(first, second):
    found = []
    for core, axis in enumerate((first, second)):
        rest = [a for a in "yxz" if a != axis]
        for others in itertools.product(range(N), repeat=2):
            at = dict(zip(rest, others))
            ring = []
            for i in range(N):
                at[axis] = i
                ring.append(((at["y"] * N + at["x"]) * N + at["z"]) * 2 + core)
            found.append(ring)
    return found


def exchange(blocks, first, second):
    return lax.all_to_all(
        blocks, AXES, 0, 0, tiled=True, axis_index_groups=groups(first, second)
    )


def mask_kernel(coef_ref, weight_ref, pattern_ref, sizes_ref, one_ref, two_ref):
    rows, width = coef_ref.shape
    wide = width // N
    core = lax.axis_index("c")
    device = ((lax.axis_index("y") * N + lax.axis_index("x")) * N + lax.axis_index("z")) * 2 + core
    block = device * rows // PAIR_ROWS
    at_row = lax.broadcasted_iota(jnp.int32, (rows, AUX_PAD), 0)
    weight = jnp.zeros((rows, AUX_PAD), jnp.float32)
    for r in range(rows):
        weight = jnp.where(at_row == r, weight_ref[r], weight)
    lane = lax.broadcasted_iota(jnp.int32, (rows, AUX_PAD), 1)
    for atom in range(width // AUX_PAD):
        size = jnp.where(pattern_ref[block, atom] > 0, sizes_ref[atom], 0)
        coef = coef_ref[:, atom * AUX_PAD : (atom + 1) * AUX_PAD].astype(jnp.float32)
        masked = jnp.where(lane < size, coef, 0.0)
        scaled = weight * masked
        to, start = divmod(atom * AUX_PAD, wide)
        columns = slice(start, start + AUX_PAD)
        one_ref[to, :, columns] = jnp.where(core == 0, masked, scaled).astype(jnp.bfloat16)
        two_ref[to, :, columns] = jnp.where(core == 0, scaled, masked).astype(jnp.bfloat16)


def masked_and_scaled(coefficients, row_weight, pattern, aux_sizes):
    rows, width = coefficients.shape
    shape = jax.ShapeDtypeStruct((N, rows, width // N), jnp.bfloat16)
    return pl.pallas_call(
        mask_kernel,
        out_shape=(shape, shape),
        in_specs=[VMEM, SMEM, SMEM, SMEM],
        out_specs=(VMEM, VMEM),
        cost_estimate=pl.CostEstimate(flops=4 * rows * width, bytes_accessed=6 * rows * width, transcendentals=0),
    )(coefficients, row_weight, pattern, aux_sizes)


def contract_kernel(one_ref, two_ref, keep_ref, send_ref):
    wide = one_ref.shape[1]
    tile = 256
    high = wide // 2
    part = keep_ref.shape[1]
    groups_in_tile = high // (2 * part)
    core = lax.axis_index("c")

    def run(left_ref, right_ref, mine, theirs):
        for m in range(2):

            def column_tile(t, carry):
                start = pl.multiple_of(t * tile, tile)
                out = lax.dot_general(
                    left_ref[:, m * high : (m + 1) * high],
                    right_ref[:, pl.ds(start, tile)],
                    (((0,), (0,)), ((), ())),
                    preferred_element_type=jnp.float32,
                ).reshape(groups_in_tile, 2, part, tile)
                at = slice(m * groups_in_tile, (m + 1) * groups_in_tile)
                keep_ref[at, :, pl.ds(start, tile)] = out[:, mine]
                send_ref[at, :, pl.ds(start, tile)] = out[:, theirs]
                return carry

            lax.fori_loop(0, wide // tile, column_tile, 0)

    @pl.when(core == 0)
    def _():
        run(one_ref, two_ref, 0, 1)

    @pl.when(core == 1)
    def _():
        run(two_ref, one_ref, 1, 0)


def contract(one, two):
    depth, wide = one.shape
    shape = jax.ShapeDtypeStruct((N, wide // (2 * N), wide), jnp.float32)
    return pl.pallas_call(
        contract_kernel,
        out_shape=(shape, shape),
        in_specs=[VMEM, VMEM],
        out_specs=(VMEM, VMEM),
        compiler_params=pltpu.CompilerParams(vmem_limit_bytes=40 * 2**20),
        cost_estimate=pl.CostEstimate(
            flops=2 * depth * wide * wide, bytes_accessed=4 * depth * wide + 4 * wide * wide, transcendentals=0
        ),
    )(one, two)


def per_device(coefficients, row_weight, pattern, aux_sizes):
    one, two = masked_and_scaled(coefficients, row_weight, pattern, aux_sizes)
    rows, wide = one.shape[1:]
    one = exchange(one, "y", "z").reshape(N * rows, wide)
    one = lax.all_gather(one, AXES, axis=0, tiled=True, axis_index_groups=groups("z", "y"))
    two = exchange(two, "z", "y").reshape(1, N * rows, wide)
    two = exchange(jnp.broadcast_to(two, (N, N * rows, wide)), "y", "z")
    two = two.reshape(N, N, rows, wide).transpose(1, 0, 2, 3).reshape(N * N * rows, wide)
    keep, send = contract(one, two)
    received = lax.ppermute(send, "c", [(0, 1), (1, 0)])
    partial_sum = (keep + received).astype(jnp.bfloat16)
    parts = lax.all_to_all(partial_sum, "x", 0, 0, tiled=True)
    return jnp.sum(parts.astype(jnp.float32), axis=0)


def solution(mesh):
    grid = Mesh(mesh.devices.reshape(N, N, N, 2), AXES)
    placed = (P(AXES, None), P(AXES), P(), P())
    return jax.shard_map(
        per_device,
        mesh=grid,
        in_specs=placed,
        out_specs=P(("y", "x", "c"), "z"),
        check_vma=False,
    )
```

```python
import itertools

import jax
import jax.numpy as jnp
from jax import lax
from jax.experimental import pallas as pl
from jax.experimental.pallas import tpu as pltpu
from jax.sharding import Mesh, PartitionSpec as P

PAIR_ROWS = 128
AUX_PAD = 128
N = 8
AXES = ("y", "x", "z", "c")
HALF = 384
ROWS = 48
STEPS = 14
SMEM = pl.BlockSpec(memory_space=pltpu.SMEM)
VMEM = pl.BlockSpec(memory_space=pltpu.VMEM)


def groups(first, second):
    found = []
    for core, axis in enumerate((first, second)):
        rest = [a for a in "yxz" if a != axis]
        for others in itertools.product(range(N), repeat=2):
            at = dict(zip(rest, others))
            ring = []
            for i in range(N):
                at[axis] = i
                ring.append(((at["y"] * N + at["x"]) * N + at["z"]) * 2 + core)
            found.append(ring)
    return found


def exchange(blocks, first, second):
    return lax.all_to_all(
        blocks, AXES, 0, 0, tiled=True, axis_index_groups=groups(first, second)
    )


def mask_kernel(coef_ref, weight_ref, pattern_ref, sizes_ref, keep_ref, send_ref):
    rows, width = coef_ref.shape
    wide = width // N
    core = lax.axis_index("c")
    device = ((lax.axis_index("y") * N + lax.axis_index("x")) * N + lax.axis_index("z")) * 2 + core
    block = device * rows // PAIR_ROWS
    at_row = lax.broadcasted_iota(jnp.int32, (rows, AUX_PAD), 0)
    weight = jnp.zeros((rows, AUX_PAD), jnp.float32)
    for r in range(rows):
        weight = jnp.where(at_row == r, weight_ref[r], weight)
    lane = lax.broadcasted_iota(jnp.int32, (rows, AUX_PAD), 1)
    for atom in range(width // AUX_PAD):
        size = jnp.where(pattern_ref[atom, block] > 0, sizes_ref[atom], 0)
        coef = coef_ref[:, atom * AUX_PAD : (atom + 1) * AUX_PAD].astype(jnp.float32)
        masked = jnp.where(lane < size, coef, 0.0)
        scaled = weight * masked
        to, start = divmod(atom * AUX_PAD, wide)
        columns = slice(start, start + AUX_PAD)
        keep_ref[to, :, columns] = jnp.where(core == 0, masked, scaled).astype(jnp.bfloat16)
        send_ref[to, :, columns] = jnp.where(core == 0, scaled, masked).astype(jnp.bfloat16)


def masked_and_scaled(coefficients, row_weight, pattern, aux_sizes):
    rows, width = coefficients.shape
    shape = jax.ShapeDtypeStruct((N, rows, width // N), jnp.bfloat16)
    return pl.pallas_call(
        mask_kernel,
        out_shape=(shape, shape),
        in_specs=[VMEM, SMEM, SMEM, SMEM],
        out_specs=(VMEM, VMEM),
        cost_estimate=pl.CostEstimate(flops=4 * rows * width, bytes_accessed=6 * rows * width, transcendentals=0),
    )(coefficients, row_weight, pattern.T, aux_sizes)


def contract_part(own_ref, other_ref, gathered, part, write):
    steps, inner, two, rows, wide = own_ref.shape
    count = other_ref.shape[0] // (steps * two * rows)
    at = 0
    for k in range(count):
        for i in range(steps):
            for h in range(two):
                gathered[at : at + rows, :] = own_ref[i, part * count + k, 1 - h]
                at += rows
    tile = 256
    core = lax.axis_index("c")

    def run(left_ref, right_ref, columns):
        def row_tile(t, carry):
            start = pl.multiple_of(t * tile, tile)
            write(
                start,
                lax.dot_general(
                    left_ref[:, pl.ds(start, tile)],
                    right_ref[:, columns],
                    (((0,), (0,)), ((), ())),
                    preferred_element_type=jnp.float32,
                ),
            )
            return carry

        lax.fori_loop(0, wide // tile, row_tile, 0)

    @pl.when(core == 0)
    def _():
        run(gathered, other_ref, slice(0, HALF))

    @pl.when(core == 1)
    def _():
        run(other_ref, gathered, slice(HALF, 2 * HALF))


def first_part_kernel(own_ref, other_ref, out_ref, gathered):
    def write(start, value):
        out_ref[pl.ds(start, value.shape[0]), :] = value

    contract_part(own_ref, other_ref, gathered, 0, write)


def second_part_kernel(own_ref, other_ref, first_ref, out_ref, gathered, total):
    def write(start, value):
        rows = pl.ds(start, value.shape[0])
        total[rows, :] = first_ref[rows, :] + value

    contract_part(own_ref, other_ref, gathered, 1, write)

    lanes = out_ref.shape[2]
    tiles = HALF // lanes
    tail = out_ref.shape[1] - tiles * ROWS
    at_row = lax.broadcasted_iota(jnp.int32, (tail, lanes), 0)

    def message(d, carry):
        block = total[pl.ds(pl.multiple_of(d * ROWS, 16), ROWS), :]
        exponents = jnp.zeros((tail, lanes), jnp.int32)
        for t in range(tiles):
            value = block[:, t * lanes : (t + 1) * lanes]
            largest = jnp.max(jnp.abs(value), axis=0, keepdims=True)
            exponent = jnp.floor(jnp.log2(jnp.maximum(largest, 2.0**-110)))
            coded = jnp.floor(value * jnp.exp2(STEPS - exponent) + 0.5)
            coded = jnp.clip(coded, -32767.0, 32767.0).astype(jnp.int32)
            out_ref[d, t * ROWS : (t + 1) * ROWS, :] = coded.astype(jnp.int16)
            exponents = jnp.where(at_row == t, exponent.astype(jnp.int32), exponents)
        out_ref[d, tiles * ROWS :, :] = exponents.astype(jnp.int16)
        return carry

    lax.fori_loop(0, out_ref.shape[0], message, 0)


def sum_kernel(parts_ref, out_ref):
    messages, _, lanes = parts_ref.shape
    tiles = HALF // lanes
    for core in range(2):
        totals = [jnp.zeros((ROWS, lanes), jnp.float32) for _ in range(tiles)]
        for d in range(core, messages, 2):
            exponents = parts_ref[d, tiles * ROWS :, :].astype(jnp.int32).astype(jnp.float32)
            for t in range(tiles):
                scale = jnp.exp2(exponents[t : t + 1, :] - STEPS)
                coded = parts_ref[d, t * ROWS : (t + 1) * ROWS, :].astype(jnp.int32)
                totals[t] = totals[t] + coded.astype(jnp.float32) * scale
        for t in range(tiles):
            start = core * HALF + t * lanes
            out_ref[:, start : start + lanes] = totals[t]


def contract(own, other, first):
    depth, wide = other.shape
    gathered = pltpu.VMEM((depth, wide), jnp.bfloat16)
    total = pltpu.VMEM((wide, HALF), jnp.float32)
    cost = pl.CostEstimate(flops=2 * depth * wide * HALF, bytes_accessed=8 * depth * wide, transcendentals=0)
    params = pltpu.CompilerParams(vmem_limit_bytes=32 * 2**20)
    if first is None:
        return pl.pallas_call(
            first_part_kernel,
            out_shape=jax.ShapeDtypeStruct((wide, HALF), jnp.float32),
            in_specs=[VMEM, VMEM],
            out_specs=VMEM,
            scratch_shapes=[gathered],
            compiler_params=params,
            cost_estimate=cost,
        )(own, other)
    lanes = 128
    return pl.pallas_call(
        second_part_kernel,
        out_shape=jax.ShapeDtypeStruct((wide // ROWS, HALF // lanes * ROWS + 16, lanes), jnp.int16),
        in_specs=[VMEM, VMEM, VMEM],
        out_specs=VMEM,
        scratch_shapes=[gathered, total],
        compiler_params=params,
        cost_estimate=cost,
    )(own, other, first)


def per_device(coefficients, row_weight, pattern, aux_sizes):
    keep, send = masked_and_scaled(coefficients, row_weight, pattern, aux_sizes)
    rows, wide = keep.shape[1:]
    swap = [(0, 1), (1, 0)]
    blocks = jnp.concatenate([keep, lax.ppermute(send, "c", swap)], axis=1)
    blocks = exchange(blocks, "y", "z").reshape(1, N * 2 * rows, wide)
    own = exchange(jnp.broadcast_to(blocks, (N, N * 2 * rows, wide)), "z", "y")
    other = [
        lax.ppermute(own[p * N // 2 : (p + 1) * N // 2], "c", swap).reshape(-1, wide)
        for p in range(2)
    ]
    own = own.reshape(N, N, 2, rows, wide)
    messages = contract(own, other[1], contract(own, other[0], None))
    parts = lax.all_to_all(messages, ("x", "c"), 0, 0, tiled=True)
    return pl.pallas_call(
        sum_kernel,
        out_shape=jax.ShapeDtypeStruct((ROWS, wide), jnp.float32),
        in_specs=[VMEM],
        out_specs=VMEM,
    )(parts)


def solution(mesh):
    grid = Mesh(mesh.devices.reshape(N, N, N, 2), AXES)
    placed = (P(AXES, None), P(AXES), P(), P())
    return jax.shard_map(
        per_device,
        mesh=grid,
        in_specs=placed,
        out_specs=P(("y", "x", "c"), "z"),
        check_vma=False,
    )
```

```python
import functools
import itertools

import jax
import jax.numpy as jnp
from jax import lax
from jax.experimental import pallas as pl
from jax.experimental.pallas import tpu as pltpu
from jax.sharding import Mesh, PartitionSpec as P

PAIR_ROWS = 128
AUX_PAD = 128
N = 8
AXES = ("y", "x", "z", "c")
HALF = 384
ROWS = 48
STEPS = 14
SMEM = pl.BlockSpec(memory_space=pltpu.SMEM)
VMEM = pl.BlockSpec(memory_space=pltpu.VMEM)


def groups(first, second):
    found = []
    for core, axis in enumerate((first, second)):
        rest = [a for a in "yxz" if a != axis]
        for others in itertools.product(range(N), repeat=2):
            at = dict(zip(rest, others))
            ring = []
            for i in range(N):
                at[axis] = i
                ring.append(((at["y"] * N + at["x"]) * N + at["z"]) * 2 + core)
            found.append(ring)
    return found


def exchange(blocks, first, second):
    return lax.all_to_all(
        blocks, AXES, 0, 0, tiled=True, axis_index_groups=groups(first, second)
    )


def into_order(tiles):
    lanes = tiles[0].shape[1]
    lane = lax.broadcasted_iota(jnp.int32, tiles[0].shape, 1)
    out = [None] * len(tiles)
    for piece in range(2 * N):
        core, x = divmod(piece, N)
        to, source = piece * ROWS, (2 * x + core) * ROWS
        end = to + ROWS
        while to < end:
            count = min(end - to, lanes - to % lanes, lanes - source % lanes)
            tile, start = divmod(to, lanes)
            rolled = tiles[source // lanes]
            if (to - source) % lanes:
                rolled = pltpu.roll(rolled, (to - source) % lanes, 1)
            out[tile] = rolled if start == 0 else jnp.where(lane >= start, rolled, out[tile])
            to, source = to + count, source + count
    return out


def mask_kernel(of_left, coef_ref, weight_ref, pattern_ref, sizes_ref, out_ref):
    rows, width = coef_ref.shape
    tiles = width // N // AUX_PAD
    core = lax.axis_index("c")
    device = ((lax.axis_index("y") * N + lax.axis_index("x")) * N + lax.axis_index("z")) * 2 + core
    block = device * rows // PAIR_ROWS
    lane = lax.broadcasted_iota(jnp.int32, (rows, AUX_PAD), 1)

    def masked_tiles(to):
        found = []
        for atom in range(to * tiles, (to + 1) * tiles):
            size = jnp.where(pattern_ref[atom, block] > 0, sizes_ref[atom], 0)
            coef = coef_ref[:, atom * AUX_PAD : (atom + 1) * AUX_PAD].astype(jnp.float32)
            found.append(jnp.where(lane < size, coef, 0.0))
        return found

    def store(to, found):
        for t in range(tiles):
            out_ref[to, 0:rows, t * AUX_PAD : (t + 1) * AUX_PAD] = found[t].astype(jnp.bfloat16)

    @pl.when(core == of_left)
    def _():
        for to in range(N):
            store(to, into_order(masked_tiles(to)))

    @pl.when(core != of_left)
    def _():
        at_row = lax.broadcasted_iota(jnp.int32, (rows, AUX_PAD), 0)
        weight = jnp.zeros((rows, AUX_PAD), jnp.float32)
        for r in range(rows):
            weight = jnp.where(at_row == r, weight_ref[r], weight)
        for to in range(N):
            store(to, [weight * m for m in masked_tiles(to)])


def operand(of_left, height, coefficients, row_weight, pattern, aux_sizes):
    rows, width = coefficients.shape
    return pl.pallas_call(
        functools.partial(mask_kernel, of_left),
        out_shape=jax.ShapeDtypeStruct((N, height, width // N), jnp.bfloat16),
        in_specs=[VMEM, SMEM, SMEM, SMEM],
        out_specs=VMEM,
        cost_estimate=pl.CostEstimate(flops=8 * rows * width, bytes_accessed=4 * rows * width, transcendentals=0),
    )(coefficients, row_weight, pattern.T, aux_sizes)


def contract_part(own_ref, other_ref, gathered, part, write):
    steps, inner, two, rows, wide = own_ref.shape
    count = other_ref.shape[0] // (steps * two * rows)
    core = lax.axis_index("c")
    tile = 256

    def gather(columns):
        at = 0
        for k in range(count):
            for i in range(steps):
                for h in range(two):
                    gathered[at : at + rows, columns] = own_ref[i, part * count + k, 1 - h, :, columns]
                    at += rows

    def run(left_ref, right_ref, columns):
        def column_tile(t, carry):
            start = pl.multiple_of(t * tile, tile)
            write(
                start,
                lax.dot_general(
                    left_ref[:, columns],
                    right_ref[:, pl.ds(start, tile)],
                    (((0,), (0,)), ((), ())),
                    preferred_element_type=jnp.float32,
                ),
            )
            return carry

        lax.fori_loop(0, wide // tile, column_tile, 0)

    @pl.when(core == 0)
    def _():
        gather(slice(0, HALF))
        run(gathered, other_ref, slice(0, HALF))

    @pl.when(core == 1)
    def _():
        gather(slice(0, wide))
        run(other_ref, gathered, slice(HALF, 2 * HALF))


def first_part_kernel(own_ref, other_ref, out_ref, gathered):
    def write(start, value):
        out_ref[:, pl.ds(start, value.shape[1])] = value

    contract_part(own_ref, other_ref, gathered, 0, write)


def second_part_kernel(own_ref, other_ref, first_ref, out_ref, gathered, total):
    def write(start, value):
        columns = pl.ds(start, value.shape[1])
        total[:, columns] = first_ref[:, columns] + value

    contract_part(own_ref, other_ref, gathered, 1, write)

    lanes = out_ref.shape[2]
    tiles = total.shape[1] // lanes
    tail = out_ref.shape[1] - tiles * ROWS
    at_row = lax.broadcasted_iota(jnp.int32, (tail, lanes), 0)

    def message(d, carry):
        rows = pl.ds(pl.multiple_of(d * ROWS, 16), ROWS)
        exponents = jnp.zeros((tail, lanes), jnp.int32)
        for t in range(tiles):
            value = total[rows, t * lanes : (t + 1) * lanes]
            largest = jnp.max(jnp.abs(value), axis=0, keepdims=True)
            exponent = jnp.floor(jnp.log2(jnp.maximum(largest, 2.0**-110)))
            coded = jnp.floor(value * jnp.exp2(STEPS - exponent) + 0.5)
            coded = jnp.clip(coded, -32767.0, 32767.0).astype(jnp.int32)
            out_ref[d, t * ROWS : (t + 1) * ROWS, :] = coded.astype(jnp.int16)
            exponents = jnp.where(at_row == t, exponent.astype(jnp.int32), exponents)
        out_ref[d, tiles * ROWS :, :] = exponents.astype(jnp.int16)
        return carry

    lax.fori_loop(0, out_ref.shape[0], message, 0)


def sum_kernel(parts_ref, out_ref):
    messages, _, lanes = parts_ref.shape
    tiles = out_ref.shape[1] // lanes
    scales = [
        jnp.exp2(parts_ref[d, tiles * ROWS :, :].astype(jnp.int32).astype(jnp.float32) - STEPS) for d in range(messages)
    ]
    for t in range(tiles):
        total = jnp.zeros((ROWS, lanes), jnp.float32)
        for d in range(messages):
            coded = parts_ref[d, t * ROWS : (t + 1) * ROWS, :].astype(jnp.int32)
            total = total + coded.astype(jnp.float32) * scales[d][t : t + 1, :]
        out_ref[:, t * lanes : (t + 1) * lanes] = total


def contract(own, other, first):
    depth, wide = other.shape
    gathered = pltpu.VMEM((depth, wide), jnp.bfloat16)
    total = pltpu.VMEM((HALF, wide), jnp.float32)
    cost = pl.CostEstimate(flops=2 * depth * wide * HALF, bytes_accessed=8 * depth * wide, transcendentals=0)
    params = pltpu.CompilerParams(vmem_limit_bytes=32 * 2**20)
    if first is None:
        return pl.pallas_call(
            first_part_kernel,
            out_shape=jax.ShapeDtypeStruct((HALF, wide), jnp.float32),
            in_specs=[VMEM, VMEM],
            out_specs=VMEM,
            scratch_shapes=[gathered],
            compiler_params=params,
            cost_estimate=cost,
        )(own, other)
    lanes = 128
    return pl.pallas_call(
        second_part_kernel,
        out_shape=jax.ShapeDtypeStruct((HALF // ROWS, wide // lanes * ROWS + 16, lanes), jnp.int16),
        in_specs=[VMEM, VMEM, VMEM],
        out_specs=VMEM,
        scratch_shapes=[gathered, total],
        compiler_params=params,
        cost_estimate=cost,
    )(own, other, first)


def per_device(coefficients, row_weight, pattern, aux_sizes):
    given = (coefficients, row_weight, pattern, aux_sizes)
    rows = coefficients.shape[0]
    swap = [(0, 1), (1, 0)]
    received = lax.ppermute(operand(1, rows, *given), "c", swap)
    blocks = lax.dynamic_update_slice(operand(0, 2 * rows, *given), received, (0, rows, 0))
    wide = blocks.shape[2]
    blocks = exchange(blocks, "y", "z").reshape(1, N * 2 * rows, wide)
    own = exchange(jnp.broadcast_to(blocks, (N, N * 2 * rows, wide)), "z", "y")
    other = [
        lax.ppermute(own[p * N // 2 : (p + 1) * N // 2], "c", swap).reshape(-1, wide)
        for p in range(2)
    ]
    own = own.reshape(N, N, 2, rows, wide)
    messages = contract(own, other[1], contract(own, other[0], None))
    parts = lax.all_to_all(messages, "x", 0, 0, tiled=True)
    return pl.pallas_call(
        sum_kernel,
        out_shape=jax.ShapeDtypeStruct((ROWS, wide), jnp.float32),
        in_specs=[VMEM],
        out_specs=VMEM,
    )(parts)


def solution(mesh):
    grid = Mesh(mesh.devices.reshape(N, N, N, 2), AXES)
    placed = (P(AXES, None), P(AXES), P(), P())
    return jax.shard_map(
        per_device,
        mesh=grid,
        in_specs=placed,
        out_specs=P(("y", "x", "c"), "z"),
        check_vma=False,
    )
```

```python
import functools
import itertools

import jax
import jax.numpy as jnp
from jax import lax
from jax.experimental import pallas as pl
from jax.experimental.pallas import tpu as pltpu
from jax.sharding import Mesh, PartitionSpec as P

PAIR_ROWS = 128
AUX_PAD = 128
N = 8
AXES = ("y", "x", "z", "c")
HALF = 384
ROWS = 48
STEPS = 14
VMEM = pl.BlockSpec(memory_space=pltpu.VMEM)
SMALL = pltpu.CompilerParams(vmem_limit_bytes=8 * 2**20)


def groups(first, second):
    found = []
    for core, axis in enumerate((first, second)):
        rest = [a for a in "yxz" if a != axis]
        for others in itertools.product(range(N), repeat=2):
            at = dict(zip(rest, others))
            ring = []
            for i in range(N):
                at[axis] = i
                ring.append(((at["y"] * N + at["x"]) * N + at["z"]) * 2 + core)
            found.append(ring)
    return found


def exchange(blocks, first, second):
    return lax.all_to_all(
        blocks, AXES, 0, 0, tiled=True, axis_index_groups=groups(first, second)
    )


def into_order(tiles):
    lanes = tiles[0].shape[1]
    lane = lax.broadcasted_iota(jnp.int32, tiles[0].shape, 1)
    out = [None] * len(tiles)
    for piece in range(2 * N):
        core, x = divmod(piece, N)
        to, source = piece * ROWS, (2 * x + core) * ROWS
        end = to + ROWS
        while to < end:
            count = min(end - to, lanes - to % lanes, lanes - source % lanes)
            tile, start = divmod(to, lanes)
            rolled = tiles[source // lanes]
            if (to - source) % lanes:
                rolled = pltpu.roll(rolled, (to - source) % lanes, 1)
            out[tile] = rolled if start == 0 else jnp.where(lane >= start, rolled, out[tile])
            to, source = to + count, source + count
    return out


def as_column(row):
    n = row.shape[1]
    square = (n, n)
    here = lax.broadcasted_iota(jnp.int32, square, 0) == lax.broadcasted_iota(jnp.int32, square, 1)
    return jnp.sum(jnp.where(here, jnp.broadcast_to(row, square), 0), axis=1, keepdims=True)


def mask_kernel(of_left, coef_ref, weight_ref, pattern_ref, sizes_ref, out_ref):
    rows, width = coef_ref.shape
    tiles = width // N // AUX_PAD
    core = lax.axis_index("c")
    device = ((lax.axis_index("y") * N + lax.axis_index("x")) * N + lax.axis_index("z")) * 2 + core
    block = device * rows // PAIR_ROWS
    lane = lax.broadcasted_iota(jnp.int32, (rows, AUX_PAD), 1)
    at_block = lax.broadcasted_iota(jnp.int32, pattern_ref.shape, 1) == block
    meets = jnp.sum(jnp.where(at_block, pattern_ref[...], 0), axis=1, keepdims=True)
    sizes = jnp.broadcast_to(jnp.where(meets > 0, as_column(sizes_ref[...]), 0), pattern_ref.shape)

    def masked_tiles(to):
        found = []
        for atom in range(to * tiles, (to + 1) * tiles):
            coef = coef_ref[:, atom * AUX_PAD : (atom + 1) * AUX_PAD].astype(jnp.float32)
            found.append(jnp.where(lane < sizes[atom : atom + 1, :], coef, 0.0))
        return found

    def store(to, found):
        for t in range(tiles):
            out_ref[to, 0:rows, t * AUX_PAD : (t + 1) * AUX_PAD] = found[t].astype(jnp.bfloat16)

    @pl.when(core == of_left)
    def _():
        for to in range(N):
            store(to, into_order(masked_tiles(to)))

    @pl.when(core != of_left)
    def _():
        weight = jnp.broadcast_to(as_column(weight_ref[...]), (rows, AUX_PAD))
        for to in range(N):
            store(to, [weight * m for m in masked_tiles(to)])


def operand(of_left, height, coefficients, row_weight, pattern, aux_sizes):
    rows, width = coefficients.shape
    return pl.pallas_call(
        functools.partial(mask_kernel, of_left),
        out_shape=jax.ShapeDtypeStruct((N, height, width // N), jnp.bfloat16),
        in_specs=[VMEM] * 4,
        out_specs=VMEM,
        compiler_params=SMALL,
        cost_estimate=pl.CostEstimate(flops=8 * rows * width, bytes_accessed=4 * rows * width, transcendentals=0),
    )(coefficients, row_weight.reshape(1, -1), pattern.T, aux_sizes.reshape(1, -1))


def contract_part(own_ref, other_ref, gathered, part, write):
    steps, inner, two, rows, wide = own_ref.shape
    count = other_ref.shape[0] // (steps * two * rows)
    core = lax.axis_index("c")
    tile = 256

    def gather(columns):
        at = 0
        for k in range(count):
            for i in range(steps):
                for h in range(two):
                    gathered[at : at + rows, columns] = own_ref[i, part * count + k, 1 - h, :, columns]
                    at += rows

    def run(left_ref, right_ref, columns):
        def column_tile(t, carry):
            start = pl.multiple_of(t * tile, tile)
            write(
                start,
                lax.dot_general(
                    left_ref[:, columns],
                    right_ref[:, pl.ds(start, tile)],
                    (((0,), (0,)), ((), ())),
                    preferred_element_type=jnp.float32,
                ),
            )
            return carry

        lax.fori_loop(0, wide // tile, column_tile, 0)

    @pl.when(core == 0)
    def _():
        gather(slice(0, HALF))
        run(gathered, other_ref, slice(0, HALF))

    @pl.when(core == 1)
    def _():
        gather(slice(0, wide))
        run(other_ref, gathered, slice(HALF, 2 * HALF))


def first_part_kernel(own_ref, other_ref, out_ref, gathered):
    def write(start, value):
        out_ref[:, pl.ds(start, value.shape[1])] = value

    contract_part(own_ref, other_ref, gathered, 0, write)


def second_part_kernel(own_ref, other_ref, first_ref, out_ref, gathered, total):
    def write(start, value):
        columns = pl.ds(start, value.shape[1])
        total[:, columns] = first_ref[:, columns] + value

    contract_part(own_ref, other_ref, gathered, 1, write)

    lanes = out_ref.shape[2]
    tiles = total.shape[1] // lanes
    tail = out_ref.shape[1] - tiles * ROWS
    at_row = lax.broadcasted_iota(jnp.int32, (tail, lanes), 0)

    def message(d, carry):
        rows = pl.ds(pl.multiple_of(d * ROWS, 16), ROWS)
        exponents = jnp.zeros((tail, lanes), jnp.int32)
        for t in range(tiles):
            value = total[rows, t * lanes : (t + 1) * lanes]
            largest = jnp.max(jnp.abs(value), axis=0, keepdims=True)
            exponent = jnp.floor(jnp.log2(jnp.maximum(largest, 2.0**-110)))
            coded = jnp.floor(value * jnp.exp2(STEPS - exponent) + 0.5)
            coded = jnp.clip(coded, -32767.0, 32767.0).astype(jnp.int32)
            out_ref[d, t * ROWS : (t + 1) * ROWS, :] = coded.astype(jnp.int16)
            exponents = jnp.where(at_row == t, exponent.astype(jnp.int32), exponents)
        out_ref[d, tiles * ROWS :, :] = exponents.astype(jnp.int16)
        return carry

    lax.fori_loop(0, out_ref.shape[0], message, 0)


def sum_kernel(parts_ref, out_ref):
    messages, _, lanes = parts_ref.shape
    tiles = out_ref.shape[1] // lanes
    scales = [
        jnp.exp2(parts_ref[d, tiles * ROWS :, :].astype(jnp.int32).astype(jnp.float32) - STEPS) for d in range(messages)
    ]
    for t in range(tiles):
        total = jnp.zeros((ROWS, lanes), jnp.float32)
        for d in range(messages):
            coded = parts_ref[d, t * ROWS : (t + 1) * ROWS, :].astype(jnp.int32)
            total = total + coded.astype(jnp.float32) * scales[d][t : t + 1, :]
        out_ref[:, t * lanes : (t + 1) * lanes] = total


def contract(own, other, first):
    depth, wide = other.shape
    gathered = pltpu.VMEM((depth, wide), jnp.bfloat16)
    total = pltpu.VMEM((HALF, wide), jnp.float32)
    cost = pl.CostEstimate(flops=2 * depth * wide * HALF, bytes_accessed=8 * depth * wide, transcendentals=0)
    params = pltpu.CompilerParams(vmem_limit_bytes=32 * 2**20)
    if first is None:
        return pl.pallas_call(
            first_part_kernel,
            out_shape=jax.ShapeDtypeStruct((HALF, wide), jnp.float32),
            in_specs=[VMEM, VMEM],
            out_specs=VMEM,
            scratch_shapes=[gathered],
            compiler_params=params,
            cost_estimate=cost,
        )(own, other)
    lanes = 128
    return pl.pallas_call(
        second_part_kernel,
        out_shape=jax.ShapeDtypeStruct((HALF // ROWS, wide // lanes * ROWS + 16, lanes), jnp.int16),
        in_specs=[VMEM, VMEM, VMEM],
        out_specs=VMEM,
        scratch_shapes=[gathered, total],
        compiler_params=params,
        cost_estimate=cost,
    )(own, other, first)


def per_device(coefficients, row_weight, pattern, aux_sizes):
    given = (coefficients, row_weight, pattern, aux_sizes)
    rows = coefficients.shape[0]
    swap = [(0, 1), (1, 0)]
    received = lax.ppermute(operand(1, rows, *given), "c", swap)
    blocks = lax.dynamic_update_slice(operand(0, 2 * rows, *given), received, (0, rows, 0))
    wide = blocks.shape[2]
    blocks = exchange(blocks, "y", "z").reshape(1, N * 2 * rows, wide)
    own = exchange(jnp.broadcast_to(blocks, (N, N * 2 * rows, wide)), "z", "y")
    other = [
        lax.ppermute(own[p * N // 2 : (p + 1) * N // 2], "c", swap).reshape(-1, wide)
        for p in range(2)
    ]
    own = own.reshape(N, N, 2, rows, wide)
    messages = contract(own, other[1], contract(own, other[0], None))
    parts = lax.all_to_all(messages, "x", 0, 0, tiled=True)
    return pl.pallas_call(
        sum_kernel,
        out_shape=jax.ShapeDtypeStruct((ROWS, wide), jnp.float32),
        in_specs=[VMEM],
        out_specs=VMEM,
        compiler_params=SMALL,
    )(parts)


def solution(mesh):
    grid = Mesh(mesh.devices.reshape(N, N, N, 2), AXES)
    placed = (P(AXES, None), P(AXES), P(), P())
    return jax.shard_map(
        per_device,
        mesh=grid,
        in_specs=placed,
        out_specs=P(("y", "x", "c"), "z"),
        check_vma=False,
    )
```

```python
import functools
import itertools

import jax
import jax.numpy as jnp
from jax import lax
from jax.experimental import pallas as pl
from jax.experimental.pallas import tpu as pltpu
from jax.sharding import Mesh, PartitionSpec as P

PAIR_ROWS = 128
AUX_PAD = 128
N = 8
AXES = ("y", "x", "z", "c")
HALF = 384
ROWS = 48
ORDER = (0, 1, 7, 2, 6, 3, 5, 4)
STEPS = 14
VMEM = pl.BlockSpec(memory_space=pltpu.VMEM)
SMALL = pltpu.CompilerParams(vmem_limit_bytes=8 * 2**20)


def groups(first, second):
    found = []
    for core, axis in enumerate((first, second)):
        rest = [a for a in "yxz" if a != axis]
        for others in itertools.product(range(N), repeat=2):
            at = dict(zip(rest, others))
            ring = []
            for i in range(N):
                at[axis] = i
                ring.append(((at["y"] * N + at["x"]) * N + at["z"]) * 2 + core)
            found.append(ring)
    return found


def exchange(blocks, first, second):
    return lax.all_to_all(
        blocks, AXES, 0, 0, tiled=True, axis_index_groups=groups(first, second)
    )


def into_order(tiles):
    lanes = tiles[0].shape[1]
    lane = lax.broadcasted_iota(jnp.int32, tiles[0].shape, 1)
    out = [None] * len(tiles)
    for piece in range(2 * N):
        core, x = divmod(piece, N)
        to, source = piece * ROWS, (2 * x + core) * ROWS
        end = to + ROWS
        while to < end:
            count = min(end - to, lanes - to % lanes, lanes - source % lanes)
            tile, start = divmod(to, lanes)
            rolled = tiles[source // lanes]
            if (to - source) % lanes:
                rolled = pltpu.roll(rolled, (to - source) % lanes, 1)
            out[tile] = rolled if start == 0 else jnp.where(lane >= start, rolled, out[tile])
            to, source = to + count, source + count
    return out


def as_column(row):
    n = row.shape[1]
    square = (n, n)
    here = lax.broadcasted_iota(jnp.int32, square, 0) == lax.broadcasted_iota(jnp.int32, square, 1)
    return jnp.sum(jnp.where(here, jnp.broadcast_to(row, square), 0), axis=1, keepdims=True)


def mask_kernel(coef_at, weight_at, pattern_at, sizes_at, send_ref, keep_ref, coef_ref, weight_ref, pattern_ref, sizes_ref, arrived):
    copies = [
        pltpu.make_async_copy(there, here, arrived.at[i])
        for i, (there, here) in enumerate(
            ((coef_at, coef_ref), (pattern_at, pattern_ref), (sizes_at, sizes_ref), (weight_at, weight_ref))
        )
    ]
    for copy in copies:
        copy.start()
    for copy in copies:
        copy.wait()
    rows, width = coef_ref.shape
    tiles = width // N // AUX_PAD
    core = lax.axis_index("c")
    device = ((lax.axis_index("y") * N + lax.axis_index("x")) * N + lax.axis_index("z")) * 2 + core
    block = device * rows // PAIR_ROWS
    lane = lax.broadcasted_iota(jnp.int32, (rows, AUX_PAD), 1)
    at_block = lax.broadcasted_iota(jnp.int32, pattern_ref.shape, 1) == block
    meets = jnp.sum(jnp.where(at_block, pattern_ref[...], 0), axis=1, keepdims=True)
    sizes = jnp.broadcast_to(jnp.where(meets > 0, as_column(sizes_ref[...]), 0), pattern_ref.shape)
    weight = jnp.broadcast_to(as_column(weight_ref[...]), (rows, AUX_PAD))

    def store(ref, to, found):
        for t in range(tiles):
            ref[to, 0:rows, t * AUX_PAD : (t + 1) * AUX_PAD] = found[t].astype(jnp.bfloat16)

    def run(left_ref, right_ref):
        for to in range(N):
            masked = []
            for atom in range(to * tiles, (to + 1) * tiles):
                coef = coef_ref[:, atom * AUX_PAD : (atom + 1) * AUX_PAD].astype(jnp.float32)
                masked.append(jnp.where(lane < sizes[atom : atom + 1, :], coef, 0.0))
            store(left_ref, to, into_order(masked))
            store(right_ref, to, [weight * m for m in masked])

    @pl.when(core == 0)
    def _():
        run(keep_ref, send_ref)

    @pl.when(core == 1)
    def _():
        run(send_ref, keep_ref)


def operands(coefficients, row_weight, pattern, aux_sizes):
    rows, width = coefficients.shape
    given = (coefficients, row_weight.reshape(1, -1), pattern.T, aux_sizes.reshape(1, -1))
    return pl.pallas_call(
        mask_kernel,
        out_shape=[jax.ShapeDtypeStruct((N, height, width // N), jnp.bfloat16) for height in (rows, 2 * rows)],
        in_specs=[pl.BlockSpec(memory_space=pltpu.HBM)] * 4,
        out_specs=[VMEM, VMEM],
        scratch_shapes=[pltpu.VMEM(g.shape, g.dtype) for g in given] + [pltpu.SemaphoreType.DMA((4,))],
        compiler_params=SMALL,
        cost_estimate=pl.CostEstimate(flops=8 * rows * width, bytes_accessed=6 * rows * width, transcendentals=0),
    )(*given)


def contract_part(own_refs, other_ref, gathered, part, write):
    slots, places, two, rows, wide = own_refs[0].shape
    core = lax.axis_index("c")
    mine = jnp.where(core == 0, lax.axis_index("z"), lax.axis_index("y"))
    theirs = jnp.where(core == 0, lax.axis_index("y"), lax.axis_index("z"))
    tile = 256

    def gather(columns):
        for k in range(slots):
            inner = lax.rem(theirs + N - ORDER[part * slots + k], N)
            for slot in range(len(ORDER)):
                place = lax.rem(mine + N - ORDER[slot], N)
                for h in range(two):
                    at = pl.multiple_of(((k * places + place) * two + h) * rows, rows)
                    gathered[pl.ds(at, rows), columns] = own_refs[slot // slots][slot % slots, inner, 1 - h, :, columns]

    def run(left_ref, right_ref, columns):
        def column_tile(t, carry):
            start = pl.multiple_of(t * tile, tile)
            write(
                start,
                lax.dot_general(
                    left_ref[:, columns],
                    right_ref[:, pl.ds(start, tile)],
                    (((0,), (0,)), ((), ())),
                    preferred_element_type=jnp.float32,
                ),
            )
            return carry

        lax.fori_loop(0, wide // tile, column_tile, 0)

    @pl.when(core == 0)
    def _():
        gather(slice(0, HALF))
        run(gathered, other_ref, slice(0, HALF))

    @pl.when(core == 1)
    def _():
        gather(slice(0, wide))
        run(other_ref, gathered, slice(HALF, 2 * HALF))


def first_part_kernel(own_0, own_1, other_ref, out_ref, gathered):
    def write(start, value):
        out_ref[:, pl.ds(start, value.shape[1])] = value

    contract_part((own_0, own_1), other_ref, gathered, 0, write)


def second_part_kernel(own_0, own_1, other_ref, first_ref, out_ref, gathered, total):
    def write(start, value):
        columns = pl.ds(start, value.shape[1])
        total[:, columns] = first_ref[:, columns] + value

    contract_part((own_0, own_1), other_ref, gathered, 1, write)

    lanes = out_ref.shape[2]
    tiles = total.shape[1] // lanes
    tail = out_ref.shape[1] - tiles * ROWS
    at_row = lax.broadcasted_iota(jnp.int32, (tail, lanes), 0)

    def message(d, carry):
        rows = pl.ds(pl.multiple_of(d * ROWS, 16), ROWS)
        exponents = jnp.zeros((tail, lanes), jnp.int32)
        for t in range(tiles):
            value = total[rows, t * lanes : (t + 1) * lanes]
            largest = jnp.max(jnp.abs(value), axis=0, keepdims=True)
            exponent = jnp.floor(jnp.log2(jnp.maximum(largest, 2.0**-110)))
            coded = jnp.floor(value * jnp.exp2(STEPS - exponent) + 0.5)
            coded = jnp.clip(coded, -32767.0, 32767.0).astype(jnp.int32)
            out_ref[d, t * ROWS : (t + 1) * ROWS, :] = coded.astype(jnp.int16)
            exponents = jnp.where(at_row == t, exponent.astype(jnp.int32), exponents)
        out_ref[d, tiles * ROWS :, :] = exponents.astype(jnp.int16)
        return carry

    lax.fori_loop(0, out_ref.shape[0], message, 0)


def sum_kernel(parts_ref, out_ref):
    messages, _, lanes = parts_ref.shape
    tiles = out_ref.shape[1] // lanes
    scales = [
        jnp.exp2(parts_ref[d, tiles * ROWS :, :].astype(jnp.int32).astype(jnp.float32) - STEPS) for d in range(messages)
    ]
    for t in range(tiles):
        total = jnp.zeros((ROWS, lanes), jnp.float32)
        for d in range(messages):
            coded = parts_ref[d, t * ROWS : (t + 1) * ROWS, :].astype(jnp.int32)
            total = total + coded.astype(jnp.float32) * scales[d][t : t + 1, :]
        out_ref[:, t * lanes : (t + 1) * lanes] = total


def contract(own, other, first):
    depth, wide = other.shape
    gathered = pltpu.VMEM((depth, wide), jnp.bfloat16)
    total = pltpu.VMEM((HALF, wide), jnp.float32)
    cost = pl.CostEstimate(flops=2 * depth * wide * HALF, bytes_accessed=8 * depth * wide, transcendentals=0)
    params = pltpu.CompilerParams(vmem_limit_bytes=32 * 2**20)
    if first is None:
        return pl.pallas_call(
            first_part_kernel,
            out_shape=jax.ShapeDtypeStruct((HALF, wide), jnp.float32),
            in_specs=[VMEM] * 3,
            out_specs=VMEM,
            scratch_shapes=[gathered],
            compiler_params=params,
            cost_estimate=cost,
        )(*own, other)
    lanes = 128
    return pl.pallas_call(
        second_part_kernel,
        out_shape=jax.ShapeDtypeStruct((HALF // ROWS, wide // lanes * ROWS + 16, lanes), jnp.int16),
        in_specs=[VMEM] * 4,
        out_specs=VMEM,
        scratch_shapes=[gathered, total],
        compiler_params=params,
        cost_estimate=cost,
    )(*own, other, first)


def along(first, second, distance):
    pairs = []
    for ring in groups(first, second):
        pairs += [(ring[i], ring[(i + distance) % N]) for i in range(N)]
    return pairs


def per_device(coefficients, row_weight, pattern, aux_sizes):
    rows = coefficients.shape[0]
    swap = [(0, 1), (1, 0)]
    send, keep = operands(coefficients, row_weight, pattern, aux_sizes)
    blocks = lax.dynamic_update_slice(keep, lax.ppermute(send, "c", swap), (0, rows, 0))
    wide = blocks.shape[2]
    blocks = exchange(blocks, "y", "z").reshape(N, 2, rows, wide)
    slots = [blocks if d == 0 else lax.ppermute(blocks, AXES, along("z", "y", d)) for d in ORDER]
    own = [jnp.stack(slots[p * N // 2 : (p + 1) * N // 2]) for p in range(2)]
    other = [lax.ppermute(part, "c", swap).reshape(-1, wide) for part in own]
    messages = contract(own, other[1], contract(own, other[0], None))
    parts = lax.all_to_all(messages, "x", 0, 0, tiled=True)
    return pl.pallas_call(
        sum_kernel,
        out_shape=jax.ShapeDtypeStruct((ROWS, wide), jnp.float32),
        in_specs=[VMEM],
        out_specs=VMEM,
        compiler_params=SMALL,
    )(parts)


def solution(mesh):
    grid = Mesh(mesh.devices.reshape(N, N, N, 2), AXES)
    placed = (P(AXES, None), P(AXES), P(), P())
    return jax.shard_map(
        per_device,
        mesh=grid,
        in_specs=placed,
        out_specs=P(("y", "x", "c"), "z"),
        check_vma=False,
    )
```

```python
import functools
import itertools

import jax
import jax.numpy as jnp
from jax import lax
from jax.experimental import pallas as pl
from jax.experimental.pallas import tpu as pltpu
from jax.sharding import Mesh, PartitionSpec as P

PAIR_ROWS = 128
AUX_PAD = 128
N = 8
AXES = ("y", "x", "z", "c")
HALF = 384
ROWS = 48
ORDER = (0, 1, 7, 2, 6, 3, 5, 4)
STEPS = 14
VMEM = pl.BlockSpec(memory_space=pltpu.VMEM)
SMALL = pltpu.CompilerParams(vmem_limit_bytes=8 * 2**20)


def groups(first, second):
    found = []
    for core, axis in enumerate((first, second)):
        rest = [a for a in "yxz" if a != axis]
        for others in itertools.product(range(N), repeat=2):
            at = dict(zip(rest, others))
            ring = []
            for i in range(N):
                at[axis] = i
                ring.append(((at["y"] * N + at["x"]) * N + at["z"]) * 2 + core)
            found.append(ring)
    return found


def exchange(blocks, first, second):
    return lax.all_to_all(
        blocks, AXES, 0, 0, tiled=True, axis_index_groups=groups(first, second)
    )


def into_order(tiles):
    lanes = tiles[0].shape[1]
    lane = lax.broadcasted_iota(jnp.int32, tiles[0].shape, 1)
    out = [None] * len(tiles)
    for piece in range(2 * N):
        core, x = divmod(piece, N)
        to, source = piece * ROWS, (2 * x + core) * ROWS
        end = to + ROWS
        while to < end:
            count = min(end - to, lanes - to % lanes, lanes - source % lanes)
            tile, start = divmod(to, lanes)
            rolled = tiles[source // lanes]
            if (to - source) % lanes:
                rolled = pltpu.roll(rolled, (to - source) % lanes, 1)
            out[tile] = rolled if start == 0 else jnp.where(lane >= start, rolled, out[tile])
            to, source = to + count, source + count
    return out


def as_column(row):
    n = row.shape[1]
    square = (n, n)
    here = lax.broadcasted_iota(jnp.int32, square, 0) == lax.broadcasted_iota(jnp.int32, square, 1)
    return jnp.sum(jnp.where(here, jnp.broadcast_to(row, square), 0.0), axis=1, keepdims=True)


def mask_kernel(coef_ref, known_ref, send_ref, keep_ref):
    rows, width = coef_ref.shape
    tiles = width // N // AUX_PAD
    core = lax.axis_index("c")
    device = ((lax.axis_index("y") * N + lax.axis_index("x")) * N + lax.axis_index("z")) * 2 + core
    block = device * rows // PAIR_ROWS
    lane = lax.broadcasted_iota(jnp.int32, (rows, AUX_PAD), 1)
    atoms = width // AUX_PAD
    pattern = known_ref[0:atoms, :]
    at_block = lax.broadcasted_iota(jnp.int32, pattern.shape, 1) == block
    meets = jnp.sum(jnp.where(at_block, pattern, 0.0), axis=1, keepdims=True)
    sizes = jnp.where(meets > 0, as_column(known_ref[atoms : atoms + 1, 0:atoms]), 0.0)
    sizes = jnp.broadcast_to(sizes, (atoms, AUX_PAD)).astype(jnp.int32)
    weight = jnp.broadcast_to(as_column(known_ref[atoms + 1 : atoms + 2, 0:rows]), (rows, AUX_PAD))

    def store(ref, to, found):
        for t in range(tiles):
            ref[to, 0:rows, t * AUX_PAD : (t + 1) * AUX_PAD] = found[t].astype(jnp.bfloat16)

    def run(left_ref, right_ref):
        for to in range(N):
            masked = []
            for atom in range(to * tiles, (to + 1) * tiles):
                coef = coef_ref[:, atom * AUX_PAD : (atom + 1) * AUX_PAD].astype(jnp.float32)
                masked.append(jnp.where(lane < sizes[atom : atom + 1, :], coef, 0.0))
            store(left_ref, to, into_order(masked))
            store(right_ref, to, [weight * m for m in masked])

    @pl.when(core == 0)
    def _():
        run(keep_ref, send_ref)

    @pl.when(core == 1)
    def _():
        run(send_ref, keep_ref)


def operands(coefficients, row_weight, pattern, aux_sizes):
    rows, width = coefficients.shape
    as_row = lambda v: jnp.pad(v.astype(jnp.float32).reshape(1, -1), ((0, 0), (0, pattern.shape[0] - v.shape[0])))
    known = jnp.concatenate([pattern.T.astype(jnp.float32), as_row(aux_sizes), as_row(row_weight)])
    return pl.pallas_call(
        mask_kernel,
        out_shape=[jax.ShapeDtypeStruct((N, height, width // N), jnp.bfloat16) for height in (rows, 2 * rows)],
        in_specs=[VMEM, VMEM],
        out_specs=[VMEM, VMEM],
        compiler_params=SMALL,
        cost_estimate=pl.CostEstimate(flops=8 * rows * width, bytes_accessed=6 * rows * width, transcendentals=0),
    )(coefficients, known)


def contract_part(own_refs, other_ref, gathered, part, write):
    slots, places, two, rows, wide = own_refs[0].shape
    core = lax.axis_index("c")
    mine = jnp.where(core == 0, lax.axis_index("z"), lax.axis_index("y"))
    theirs = jnp.where(core == 0, lax.axis_index("y"), lax.axis_index("z"))
    tile = 256

    def gather(columns):
        for k in range(slots):
            inner = lax.rem(theirs + N - ORDER[part * slots + k], N)
            for slot in range(len(ORDER)):
                place = lax.rem(mine + N - ORDER[slot], N)
                for h in range(two):
                    at = pl.multiple_of(((k * places + place) * two + h) * rows, rows)
                    gathered[pl.ds(at, rows), columns] = own_refs[slot // slots][slot % slots, inner, 1 - h, :, columns]

    def run(left_ref, right_ref, columns):
        def column_tile(t, carry):
            start = pl.multiple_of(t * tile, tile)
            write(
                start,
                lax.dot_general(
                    left_ref[:, columns],
                    right_ref[:, pl.ds(start, tile)],
                    (((0,), (0,)), ((), ())),
                    preferred_element_type=jnp.float32,
                ),
            )
            return carry

        lax.fori_loop(0, wide // tile, column_tile, 0)

    @pl.when(core == 0)
    def _():
        gather(slice(0, HALF))
        run(gathered, other_ref, slice(0, HALF))

    @pl.when(core == 1)
    def _():
        gather(slice(0, wide))
        run(other_ref, gathered, slice(HALF, 2 * HALF))


def first_part_kernel(own_0, own_1, other_ref, out_ref, gathered):
    def write(start, value):
        out_ref[:, pl.ds(start, value.shape[1])] = value

    contract_part((own_0, own_1), other_ref, gathered, 0, write)


def second_part_kernel(own_0, own_1, other_ref, first_ref, out_ref, gathered, total):
    def write(start, value):
        columns = pl.ds(start, value.shape[1])
        total[:, columns] = first_ref[:, columns] + value

    contract_part((own_0, own_1), other_ref, gathered, 1, write)

    lanes = out_ref.shape[2]
    tiles = total.shape[1] // lanes
    tail = out_ref.shape[1] - tiles * ROWS
    at_row = lax.broadcasted_iota(jnp.int32, (tail, lanes), 0)

    def message(d, carry):
        rows = pl.ds(pl.multiple_of(d * ROWS, 16), ROWS)
        exponents = jnp.zeros((tail, lanes), jnp.int32)
        for t in range(tiles):
            value = total[rows, t * lanes : (t + 1) * lanes]
            largest = jnp.max(jnp.abs(value), axis=0, keepdims=True)
            exponent = jnp.floor(jnp.log2(jnp.maximum(largest, 2.0**-110)))
            coded = jnp.floor(value * jnp.exp2(STEPS - exponent) + 0.5)
            coded = jnp.clip(coded, -32767.0, 32767.0).astype(jnp.int32)
            out_ref[d, t * ROWS : (t + 1) * ROWS, :] = coded.astype(jnp.int16)
            exponents = jnp.where(at_row == t, exponent.astype(jnp.int32), exponents)
        out_ref[d, tiles * ROWS :, :] = exponents.astype(jnp.int16)
        return carry

    lax.fori_loop(0, out_ref.shape[0], message, 0)


def sum_kernel(parts_ref, out_ref):
    messages, _, lanes = parts_ref.shape
    tiles = out_ref.shape[1] // lanes
    scales = [
        jnp.exp2(parts_ref[d, tiles * ROWS :, :].astype(jnp.int32).astype(jnp.float32) - STEPS) for d in range(messages)
    ]
    for t in range(tiles):
        total = jnp.zeros((ROWS, lanes), jnp.float32)
        for d in range(messages):
            coded = parts_ref[d, t * ROWS : (t + 1) * ROWS, :].astype(jnp.int32)
            total = total + coded.astype(jnp.float32) * scales[d][t : t + 1, :]
        out_ref[:, t * lanes : (t + 1) * lanes] = total


def contract(own, other, first):
    depth, wide = other.shape
    gathered = pltpu.VMEM((depth, wide), jnp.bfloat16)
    total = pltpu.VMEM((HALF, wide), jnp.float32)
    cost = pl.CostEstimate(flops=2 * depth * wide * HALF, bytes_accessed=8 * depth * wide, transcendentals=0)
    params = pltpu.CompilerParams(vmem_limit_bytes=32 * 2**20)
    if first is None:
        return pl.pallas_call(
            first_part_kernel,
            out_shape=jax.ShapeDtypeStruct((HALF, wide), jnp.float32),
            in_specs=[VMEM] * 3,
            out_specs=VMEM,
            scratch_shapes=[gathered],
            compiler_params=params,
            cost_estimate=cost,
        )(*own, other)
    lanes = 128
    return pl.pallas_call(
        second_part_kernel,
        out_shape=jax.ShapeDtypeStruct((HALF // ROWS, wide // lanes * ROWS + 16, lanes), jnp.int16),
        in_specs=[VMEM] * 4,
        out_specs=VMEM,
        scratch_shapes=[gathered, total],
        compiler_params=params,
        cost_estimate=cost,
    )(*own, other, first)


def along(first, second, distance):
    pairs = []
    for ring in groups(first, second):
        pairs += [(ring[i], ring[(i + distance) % N]) for i in range(N)]
    return pairs


def per_device(coefficients, row_weight, pattern, aux_sizes):
    rows = coefficients.shape[0]
    swap = [(0, 1), (1, 0)]
    send, keep = operands(coefficients, row_weight, pattern, aux_sizes)
    blocks = lax.dynamic_update_slice(keep, lax.ppermute(send, "c", swap), (0, rows, 0))
    wide = blocks.shape[2]
    blocks = exchange(blocks, "y", "z").reshape(N, 2, rows, wide)
    move = lambda value, d: lax.ppermute(value, AXES, along("z", "y", d))
    slot = {0: blocks, 2: move(blocks, 2), 6: move(blocks, -2), 1: move(blocks, 1), 7: move(blocks, -1)}
    slot[3], slot[5] = move(slot[2], 1), move(slot[6], -1)
    slot[4] = jnp.concatenate([move(slot[2][: N // 2], 2), move(slot[6][N // 2 :], -2)])
    own = [jnp.stack([slot[d] for d in ORDER[p * N // 2 : (p + 1) * N // 2]]) for p in range(2)]
    other = [lax.ppermute(part, "c", swap).reshape(-1, wide) for part in own]
    messages = contract(own, other[1], contract(own, other[0], None))
    parts = lax.all_to_all(messages, "x", 0, 0, tiled=True)
    return pl.pallas_call(
        sum_kernel,
        out_shape=jax.ShapeDtypeStruct((ROWS, wide), jnp.float32),
        in_specs=[VMEM],
        out_specs=VMEM,
        compiler_params=SMALL,
    )(parts)


def solution(mesh):
    grid = Mesh(mesh.devices.reshape(N, N, N, 2), AXES)
    placed = (P(AXES, None), P(AXES), P(), P())
    return jax.shard_map(
        per_device,
        mesh=grid,
        in_specs=placed,
        out_specs=P(("y", "x", "c"), "z"),
        check_vma=False,
    )
```

```python
import functools
import itertools

import jax
import jax.numpy as jnp
from jax import lax
from jax.experimental import pallas as pl
from jax.experimental.pallas import tpu as pltpu
from jax.sharding import Mesh, PartitionSpec as P

PAIR_ROWS = 128
AUX_PAD = 128
N = 8
AXES = ("y", "x", "z", "c")
HALF = 384
ROWS = 48
ORDER = (0, 1, 7, 2, 6, 3, 5, 4)
PARTS = ((0, 5), (5, 8))
STEPS = 14
VMEM = pl.BlockSpec(memory_space=pltpu.VMEM)
SMALL = pltpu.CompilerParams(vmem_limit_bytes=8 * 2**20)


def groups(first, second):
    found = []
    for core, axis in enumerate((first, second)):
        rest = [a for a in "yxz" if a != axis]
        for others in itertools.product(range(N), repeat=2):
            at = dict(zip(rest, others))
            ring = []
            for i in range(N):
                at[axis] = i
                ring.append(((at["y"] * N + at["x"]) * N + at["z"]) * 2 + core)
            found.append(ring)
    return found


def exchange(blocks, first, second):
    return lax.all_to_all(
        blocks, AXES, 0, 0, tiled=True, axis_index_groups=groups(first, second)
    )


def into_order(tiles):
    lanes = tiles[0].shape[1]
    lane = lax.broadcasted_iota(jnp.int32, tiles[0].shape, 1)
    out = [None] * len(tiles)
    for piece in range(2 * N):
        core, x = divmod(piece, N)
        to, source = piece * ROWS, (2 * x + core) * ROWS
        end = to + ROWS
        while to < end:
            count = min(end - to, lanes - to % lanes, lanes - source % lanes)
            tile, start = divmod(to, lanes)
            rolled = tiles[source // lanes]
            if (to - source) % lanes:
                rolled = pltpu.roll(rolled, (to - source) % lanes, 1)
            out[tile] = rolled if start == 0 else jnp.where(lane >= start, rolled, out[tile])
            to, source = to + count, source + count
    return out


def as_column(row):
    n = row.shape[1]
    square = (n, n)
    here = lax.broadcasted_iota(jnp.int32, square, 0) == lax.broadcasted_iota(jnp.int32, square, 1)
    return jnp.sum(jnp.where(here, jnp.broadcast_to(row, square), 0.0), axis=1, keepdims=True)


def mask_kernel(coef_ref, limits_ref, weight_ref, send_ref, keep_ref):
    rows, width = coef_ref.shape
    tiles = width // N // AUX_PAD
    core = lax.axis_index("c")
    device = ((lax.axis_index("y") * N + lax.axis_index("x")) * N + lax.axis_index("z")) * 2 + core
    block = device * rows // PAIR_ROWS
    lane = lax.broadcasted_iota(jnp.int32, (rows, AUX_PAD), 1)
    at_block = lax.broadcasted_iota(jnp.int32, limits_ref.shape, 1) == block
    limits = jnp.sum(jnp.where(at_block, limits_ref[...], 0), axis=1, keepdims=True)
    limits = jnp.broadcast_to(limits, limits_ref.shape)
    weight = jnp.broadcast_to(as_column(weight_ref[...]), (rows, AUX_PAD))

    def store(ref, to, found):
        for t in range(tiles):
            ref[to, 0:rows, t * AUX_PAD : (t + 1) * AUX_PAD] = found[t].astype(jnp.bfloat16)

    def run(left_ref, right_ref):
        for to in range(N):
            masked = []
            for atom in range(to * tiles, (to + 1) * tiles):
                coef = coef_ref[:, atom * AUX_PAD : (atom + 1) * AUX_PAD].astype(jnp.float32)
                masked.append(jnp.where(lane < limits[atom : atom + 1, :], coef, 0.0))
            store(left_ref, to, into_order(masked))
            store(right_ref, to, [weight * m for m in masked])

    @pl.when(core == 0)
    def _():
        run(keep_ref, send_ref)

    @pl.when(core == 1)
    def _():
        run(send_ref, keep_ref)


def operands(coefficients, row_weight, pattern, aux_sizes):
    rows, width = coefficients.shape
    limits = pattern.T * aux_sizes[:, None]
    return pl.pallas_call(
        mask_kernel,
        out_shape=[jax.ShapeDtypeStruct((N, height, width // N), jnp.bfloat16) for height in (rows, 2 * rows)],
        in_specs=[VMEM] * 3,
        out_specs=[VMEM] * 2,
        compiler_params=SMALL,
        cost_estimate=pl.CostEstimate(flops=8 * rows * width, bytes_accessed=6 * rows * width, transcendentals=0),
    )(coefficients, limits, row_weight.reshape(1, -1))


def contract_part(own_refs, other_ref, gathered, part, write):
    places, two, rows, wide = own_refs[0].shape[1:]
    core = lax.axis_index("c")
    mine = jnp.where(core == 0, lax.axis_index("z"), lax.axis_index("y"))
    theirs = jnp.where(core == 0, lax.axis_index("y"), lax.axis_index("z"))
    tile = 256

    def gather(columns):
        for k, distance in enumerate(ORDER[slice(*PARTS[part])]):
            inner = lax.rem(theirs + N - distance, N)
            for own_ref, (first, last) in zip(own_refs, PARTS):
                for slot in range(first, last):
                    place = lax.rem(mine + N - ORDER[slot], N)
                    for h in range(two):
                        at = pl.multiple_of(((k * places + place) * two + h) * rows, rows)
                        gathered[pl.ds(at, rows), columns] = own_ref[slot - first, inner, 1 - h, :, columns]

    def run(left_ref, right_ref, columns):
        def column_tile(t, carry):
            start = pl.multiple_of(t * tile, tile)
            write(
                start,
                lax.dot_general(
                    left_ref[:, columns],
                    right_ref[:, pl.ds(start, tile)],
                    (((0,), (0,)), ((), ())),
                    preferred_element_type=jnp.float32,
                ),
            )
            return carry

        lax.fori_loop(0, wide // tile, column_tile, 0)

    @pl.when(core == 0)
    def _():
        gather(slice(0, HALF))
        run(gathered, other_ref, slice(0, HALF))

    @pl.when(core == 1)
    def _():
        gather(slice(0, wide))
        run(other_ref, gathered, slice(HALF, 2 * HALF))


def first_part_kernel(own_0, own_1, other_ref, out_ref, gathered):
    def write(start, value):
        out_ref[:, pl.ds(start, value.shape[1])] = value

    contract_part((own_0, own_1), other_ref, gathered, 0, write)


def second_part_kernel(own_0, own_1, other_ref, first_ref, out_ref, gathered, total):
    def write(start, value):
        columns = pl.ds(start, value.shape[1])
        total[:, columns] = first_ref[:, columns] + value

    contract_part((own_0, own_1), other_ref, gathered, 1, write)

    lanes = out_ref.shape[2]
    tiles = total.shape[1] // lanes
    tail = out_ref.shape[1] - tiles * ROWS
    at_row = lax.broadcasted_iota(jnp.int32, (tail, lanes), 0)

    def message(d, carry):
        rows = pl.ds(pl.multiple_of(d * ROWS, 16), ROWS)
        exponents = jnp.zeros((tail, lanes), jnp.int32)
        for t in range(tiles):
            value = total[rows, t * lanes : (t + 1) * lanes]
            largest = jnp.max(jnp.abs(value), axis=0, keepdims=True)
            exponent = jnp.floor(jnp.log2(jnp.maximum(largest, 2.0**-110)))
            coded = jnp.floor(value * jnp.exp2(STEPS - exponent) + 0.5)
            coded = jnp.clip(coded, -32767.0, 32767.0).astype(jnp.int32)
            out_ref[d, t * ROWS : (t + 1) * ROWS, :] = coded.astype(jnp.int16)
            exponents = jnp.where(at_row == t, exponent.astype(jnp.int32), exponents)
        out_ref[d, tiles * ROWS :, :] = exponents.astype(jnp.int16)
        return carry

    lax.fori_loop(0, out_ref.shape[0], message, 0)


def sum_kernel(parts_ref, out_ref):
    messages, _, lanes = parts_ref.shape
    tiles = out_ref.shape[1] // lanes
    scales = [
        jnp.exp2(parts_ref[d, tiles * ROWS :, :].astype(jnp.int32).astype(jnp.float32) - STEPS) for d in range(messages)
    ]
    for t in range(tiles):
        total = jnp.zeros((ROWS, lanes), jnp.float32)
        for d in range(messages):
            coded = parts_ref[d, t * ROWS : (t + 1) * ROWS, :].astype(jnp.int32)
            total = total + coded.astype(jnp.float32) * scales[d][t : t + 1, :]
        out_ref[:, t * lanes : (t + 1) * lanes] = total


def contract(own, other, first):
    depth, wide = other.shape
    gathered = pltpu.VMEM((depth, wide), jnp.bfloat16)
    total = pltpu.VMEM((HALF, wide), jnp.float32)
    cost = pl.CostEstimate(flops=2 * depth * wide * HALF, bytes_accessed=8 * depth * wide, transcendentals=0)
    params = pltpu.CompilerParams(vmem_limit_bytes=32 * 2**20)
    if first is None:
        return pl.pallas_call(
            first_part_kernel,
            out_shape=jax.ShapeDtypeStruct((HALF, wide), jnp.float32),
            in_specs=[VMEM] * 3,
            out_specs=VMEM,
            scratch_shapes=[gathered],
            compiler_params=params,
            cost_estimate=cost,
        )(*own, other)
    lanes = 128
    return pl.pallas_call(
        second_part_kernel,
        out_shape=jax.ShapeDtypeStruct((HALF // ROWS, wide // lanes * ROWS + 16, lanes), jnp.int16),
        in_specs=[VMEM] * 4,
        out_specs=VMEM,
        scratch_shapes=[gathered, total],
        compiler_params=params,
        cost_estimate=cost,
    )(*own, other, first)


def along(first, second, distance):
    pairs = []
    for ring in groups(first, second):
        pairs += [(ring[i], ring[(i + distance) % N]) for i in range(N)]
    return pairs


def per_device(coefficients, row_weight, pattern, aux_sizes):
    rows = coefficients.shape[0]
    swap = [(0, 1), (1, 0)]
    send, keep = operands(coefficients, row_weight, pattern, aux_sizes)
    blocks = lax.dynamic_update_slice(keep, lax.ppermute(send, "c", swap), (0, rows, 0))
    wide = blocks.shape[2]
    blocks = exchange(blocks, "y", "z").reshape(N, 2, rows, wide)
    move = lambda value, d: lax.ppermute(value, AXES, along("z", "y", d))
    slot = {0: blocks, 2: move(blocks, 2), 6: move(blocks, -2), 1: move(blocks, 1), 7: move(blocks, -1)}
    slot[3], slot[5] = move(slot[2], 1), move(slot[6], -1)
    slot[4] = jnp.concatenate([move(slot[2][: N // 2], 2), move(slot[6][N // 2 :], -2)])
    own = [jnp.stack([slot[d] for d in ORDER[slice(*part)]]) for part in PARTS]
    other = [lax.ppermute(part, "c", swap).reshape(-1, wide) for part in own]
    messages = contract(own, other[1], contract(own, other[0], None))
    parts = lax.all_to_all(messages, "x", 0, 0, tiled=True)
    return pl.pallas_call(
        sum_kernel,
        out_shape=jax.ShapeDtypeStruct((ROWS, wide), jnp.float32),
        in_specs=[VMEM],
        out_specs=VMEM,
        compiler_params=SMALL,
    )(parts)


def solution(mesh):
    grid = Mesh(mesh.devices.reshape(N, N, N, 2), AXES)
    placed = (P(AXES, None), P(AXES), P(), P())
    return jax.shard_map(
        per_device,
        mesh=grid,
        in_specs=placed,
        out_specs=P(("y", "x", "c"), "z"),
        check_vma=False,
    )
```

```python
import functools
import itertools

import jax
import jax.numpy as jnp
from jax import lax
from jax.experimental import pallas as pl
from jax.experimental.pallas import tpu as pltpu
from jax.sharding import Mesh, PartitionSpec as P

PAIR_ROWS = 128
AUX_PAD = 128
N = 8
AXES = ("y", "x", "z", "c")
HALF = 384
ROWS = 48
ORDER = (0, 2, 6, 1, 7, 3, 5, 4)
PARTS = ((0, 4), (4, 8))
STEPS = 14
VMEM = pl.BlockSpec(memory_space=pltpu.VMEM)
SMALL = pltpu.CompilerParams(vmem_limit_bytes=8 * 2**20)


def groups(first, second):
    found = []
    for core, axis in enumerate((first, second)):
        rest = [a for a in "yxz" if a != axis]
        for others in itertools.product(range(N), repeat=2):
            at = dict(zip(rest, others))
            ring = []
            for i in range(N):
                at[axis] = i
                ring.append(((at["y"] * N + at["x"]) * N + at["z"]) * 2 + core)
            found.append(ring)
    return found


def exchange(blocks, first, second):
    return lax.all_to_all(
        blocks, AXES, 0, 0, tiled=True, axis_index_groups=groups(first, second)
    )


def into_order(tiles):
    lanes = tiles[0].shape[1]
    lane = lax.broadcasted_iota(jnp.int32, tiles[0].shape, 1)
    out = [None] * len(tiles)
    for piece in range(2 * N):
        core, x = divmod(piece, N)
        to, source = piece * ROWS, (2 * x + core) * ROWS
        end = to + ROWS
        while to < end:
            count = min(end - to, lanes - to % lanes, lanes - source % lanes)
            tile, start = divmod(to, lanes)
            rolled = tiles[source // lanes]
            if (to - source) % lanes:
                rolled = pltpu.roll(rolled, (to - source) % lanes, 1)
            out[tile] = rolled if start == 0 else jnp.where(lane >= start, rolled, out[tile])
            to, source = to + count, source + count
    return out


def as_column(row):
    n = row.shape[1]
    square = (n, n)
    here = lax.broadcasted_iota(jnp.int32, square, 0) == lax.broadcasted_iota(jnp.int32, square, 1)
    return jnp.sum(jnp.where(here, jnp.broadcast_to(row, square), 0.0), axis=1, keepdims=True)


def mask_kernel(coef_ref, limits_ref, weight_ref, send_ref, keep_ref):
    rows, width = coef_ref.shape
    tiles = width // N // AUX_PAD
    core = lax.axis_index("c")
    device = ((lax.axis_index("y") * N + lax.axis_index("x")) * N + lax.axis_index("z")) * 2 + core
    block = device * rows // PAIR_ROWS
    lane = lax.broadcasted_iota(jnp.int32, (rows, AUX_PAD), 1)
    at_block = lax.broadcasted_iota(jnp.int32, limits_ref.shape, 1) == block
    limits = jnp.sum(jnp.where(at_block, limits_ref[...], 0), axis=1, keepdims=True)
    limits = jnp.broadcast_to(limits, limits_ref.shape)
    weight = jnp.broadcast_to(as_column(weight_ref[...]), (rows, AUX_PAD))

    def store(ref, to, found):
        for t in range(tiles):
            ref[to, 0:rows, t * AUX_PAD : (t + 1) * AUX_PAD] = found[t].astype(jnp.bfloat16)

    def run(left_ref, right_ref):
        for to in range(N):
            masked = []
            for atom in range(to * tiles, (to + 1) * tiles):
                coef = coef_ref[:, atom * AUX_PAD : (atom + 1) * AUX_PAD].astype(jnp.float32)
                masked.append(jnp.where(lane < limits[atom : atom + 1, :], coef, 0.0))
            store(left_ref, to, into_order(masked))
            store(right_ref, to, [weight * m for m in masked])

    @pl.when(core == 0)
    def _():
        run(keep_ref, send_ref)

    @pl.when(core == 1)
    def _():
        run(send_ref, keep_ref)


def operands(coefficients, row_weight, pattern, aux_sizes):
    rows, width = coefficients.shape
    limits = pattern.T * aux_sizes[:, None]
    return pl.pallas_call(
        mask_kernel,
        out_shape=[jax.ShapeDtypeStruct((N, height, width // N), jnp.bfloat16) for height in (rows, 2 * rows)],
        in_specs=[VMEM] * 3,
        out_specs=[VMEM] * 2,
        compiler_params=SMALL,
        cost_estimate=pl.CostEstimate(flops=8 * rows * width, bytes_accessed=6 * rows * width, transcendentals=0),
    )(coefficients, limits, row_weight.reshape(1, -1))


def contract_part(own_refs, other_ref, gathered, part, write):
    places, two, rows, wide = own_refs[0].shape[1:]
    core = lax.axis_index("c")
    mine = jnp.where(core == 0, lax.axis_index("z"), lax.axis_index("y"))
    theirs = jnp.where(core == 0, lax.axis_index("y"), lax.axis_index("z"))
    tile = 256

    def gather(columns):
        for k, distance in enumerate(ORDER[slice(*PARTS[part])]):
            inner = lax.rem(theirs + N - distance, N)
            for own_ref, (first, last) in zip(own_refs, PARTS):
                for slot in range(first, last):
                    place = lax.rem(mine + N - ORDER[slot], N)
                    for h in range(two):
                        at = pl.multiple_of(((k * places + place) * two + h) * rows, rows)
                        gathered[pl.ds(at, rows), columns] = own_ref[slot - first, inner, 1 - h, :, columns]

    depth = other_ref.shape[0]

    def run(left_ref, right_ref, columns):
        def column_tile(t, carry):
            start = pl.multiple_of(t * tile, tile)
            write(
                start,
                lax.dot_general(
                    left_ref[0:depth, columns],
                    right_ref[0:depth, pl.ds(start, tile)],
                    (((0,), (0,)), ((), ())),
                    preferred_element_type=jnp.float32,
                ),
            )
            return carry

        lax.fori_loop(0, wide // tile, column_tile, 0)

    @pl.when(core == 0)
    def _():
        gather(slice(0, HALF))
        run(gathered, other_ref, slice(0, HALF))

    @pl.when(core == 1)
    def _():
        gather(slice(0, wide))
        run(other_ref, gathered, slice(HALF, 2 * HALF))


def contract_parts(parts, own_refs, other_refs, sum_ref, out_ref, gathered):
    for part, other_ref in zip(parts, other_refs):

        def write(start, value, before=sum_ref):
            columns = pl.ds(start, value.shape[1])
            out_ref[:, columns] = value if before is None else before[:, columns] + value

        contract_part(own_refs, other_ref, gathered, part, write)
        sum_ref = out_ref


def first_parts_kernel(parts, *refs):
    own, other, (out_ref, gathered) = refs[: len(PARTS)], refs[len(PARTS) : -2], refs[-2:]
    contract_parts(parts, own, other, None, out_ref, gathered)


def last_part_kernel(parts, *refs):
    own, other, (first_ref, out_ref, gathered, total) = refs[: len(PARTS)], refs[len(PARTS) : -4], refs[-4:]
    contract_parts(parts, own, other, first_ref, total, gathered)

    lanes = out_ref.shape[2]
    tiles = total.shape[1] // lanes
    tail = out_ref.shape[1] - tiles * ROWS
    at_row = lax.broadcasted_iota(jnp.int32, (tail, lanes), 0)

    def message(d, carry):
        rows = pl.ds(pl.multiple_of(d * ROWS, 16), ROWS)
        exponents = jnp.zeros((tail, lanes), jnp.int32)
        for t in range(tiles):
            value = total[rows, t * lanes : (t + 1) * lanes]
            largest = jnp.max(jnp.abs(value), axis=0, keepdims=True)
            exponent = jnp.floor(jnp.log2(jnp.maximum(largest, 2.0**-110)))
            coded = jnp.floor(value * jnp.exp2(STEPS - exponent) + 0.5)
            coded = jnp.clip(coded, -32767.0, 32767.0).astype(jnp.int32)
            out_ref[d, t * ROWS : (t + 1) * ROWS, :] = coded.astype(jnp.int16)
            exponents = jnp.where(at_row == t, exponent.astype(jnp.int32), exponents)
        out_ref[d, tiles * ROWS :, :] = exponents.astype(jnp.int16)
        return carry

    lax.fori_loop(0, out_ref.shape[0], message, 0)


def sum_kernel(parts_ref, out_ref):
    messages, _, lanes = parts_ref.shape
    tiles = out_ref.shape[1] // lanes
    scales = [
        jnp.exp2(parts_ref[d, tiles * ROWS :, :].astype(jnp.int32).astype(jnp.float32) - STEPS) for d in range(messages)
    ]
    for t in range(tiles):
        total = jnp.zeros((ROWS, lanes), jnp.float32)
        for d in range(messages):
            coded = parts_ref[d, t * ROWS : (t + 1) * ROWS, :].astype(jnp.int32)
            total = total + coded.astype(jnp.float32) * scales[d][t : t + 1, :]
        out_ref[:, t * lanes : (t + 1) * lanes] = total


def contract(own, other):
    wide = own[0].shape[-1]
    *early, last = range(len(PARTS))
    depths = [o.shape[0] for o in other]
    gathered = lambda parts: pltpu.VMEM((max(depths[p] for p in parts), wide), jnp.bfloat16)
    cost = lambda parts: pl.CostEstimate(
        flops=2 * sum(depths[p] for p in parts) * wide * HALF,
        bytes_accessed=8 * sum(depths[p] for p in parts) * wide,
        transcendentals=0,
    )
    params = pltpu.CompilerParams(vmem_limit_bytes=32 * 2**20)
    first = pl.pallas_call(
        functools.partial(first_parts_kernel, early),
        out_shape=jax.ShapeDtypeStruct((HALF, wide), jnp.float32),
        in_specs=[VMEM] * (len(PARTS) + len(early)),
        out_specs=VMEM,
        scratch_shapes=[gathered(early)],
        compiler_params=params,
        cost_estimate=cost(early),
    )(*own, *[other[p] for p in early])
    lanes = 128
    return pl.pallas_call(
        functools.partial(last_part_kernel, [last]),
        out_shape=jax.ShapeDtypeStruct((HALF // ROWS, wide // lanes * ROWS + 16, lanes), jnp.int16),
        in_specs=[VMEM] * (len(PARTS) + 2),
        out_specs=VMEM,
        scratch_shapes=[gathered([last]), pltpu.VMEM((HALF, wide), jnp.float32)],
        compiler_params=params,
        cost_estimate=cost([last]),
    )(*own, other[last], first)


def along(first, second, distance):
    pairs = []
    for ring in groups(first, second):
        pairs += [(ring[i], ring[(i + distance) % N]) for i in range(N)]
    return pairs


def per_device(coefficients, row_weight, pattern, aux_sizes):
    rows = coefficients.shape[0]
    swap = [(0, 1), (1, 0)]
    send, keep = operands(coefficients, row_weight, pattern, aux_sizes)
    blocks = lax.dynamic_update_slice(keep, lax.ppermute(send, "c", swap), (0, rows, 0))
    wide = blocks.shape[2]
    blocks = exchange(blocks, "y", "z").reshape(N, 2, rows, wide)
    move = lambda value, d: lax.ppermute(value, AXES, along("z", "y", d))
    slot = {0: blocks, 2: move(blocks, 2), 6: move(blocks, -2), 1: move(blocks, 1), 7: move(blocks, -1)}
    slot[3], slot[5] = move(slot[2], 1), move(slot[6], -1)
    slot[4] = jnp.concatenate([move(slot[2][: N // 2], 2), move(slot[6][N // 2 :], -2)])
    own = [jnp.stack([slot[d] for d in ORDER[slice(*part)]]) for part in PARTS]
    other = [lax.ppermute(part, "c", swap).reshape(-1, wide) for part in own]
    messages = contract(own, other)
    parts = lax.all_to_all(messages, "x", 0, 0, tiled=True)
    return pl.pallas_call(
        sum_kernel,
        out_shape=jax.ShapeDtypeStruct((ROWS, wide), jnp.float32),
        in_specs=[VMEM],
        out_specs=VMEM,
        compiler_params=SMALL,
    )(parts)


def solution(mesh):
    grid = Mesh(mesh.devices.reshape(N, N, N, 2), AXES)
    placed = (P(AXES, None), P(AXES), P(), P())
    return jax.shard_map(
        per_device,
        mesh=grid,
        in_specs=placed,
        out_specs=P(("y", "x", "c"), "z"),
        check_vma=False,
    )
```

```python
import functools
import itertools

import jax
import jax.numpy as jnp
from jax import lax
from jax.experimental import pallas as pl
from jax.experimental.pallas import tpu as pltpu
from jax.sharding import Mesh, PartitionSpec as P

PAIR_ROWS = 128
AUX_PAD = 128
N = 8
AXES = ("y", "x", "z", "c")
HALF = 384
ROWS = 48
ORDER = (0, 2, 6, 4, 1, 7, 3, 5)
PARTS = ((0, 4), (4, 8))
STEPS = 14
VMEM = pl.BlockSpec(memory_space=pltpu.VMEM)
SMALL = pltpu.CompilerParams(vmem_limit_bytes=8 * 2**20)


def groups(first, second):
    found = []
    for core, axis in enumerate((first, second)):
        rest = [a for a in "yxz" if a != axis]
        for others in itertools.product(range(N), repeat=2):
            at = dict(zip(rest, others))
            ring = []
            for i in range(N):
                at[axis] = i
                ring.append(((at["y"] * N + at["x"]) * N + at["z"]) * 2 + core)
            found.append(ring)
    return found


def exchange(blocks, first, second):
    return lax.all_to_all(
        blocks, AXES, 0, 0, tiled=True, axis_index_groups=groups(first, second)
    )


def into_order(tiles):
    lanes = tiles[0].shape[1]
    lane = lax.broadcasted_iota(jnp.int32, tiles[0].shape, 1)
    out = [None] * len(tiles)
    for piece in range(2 * N):
        core, x = divmod(piece, N)
        to, source = piece * ROWS, (2 * x + core) * ROWS
        end = to + ROWS
        while to < end:
            count = min(end - to, lanes - to % lanes, lanes - source % lanes)
            tile, start = divmod(to, lanes)
            rolled = tiles[source // lanes]
            if (to - source) % lanes:
                rolled = pltpu.roll(rolled, (to - source) % lanes, 1)
            out[tile] = rolled if start == 0 else jnp.where(lane >= start, rolled, out[tile])
            to, source = to + count, source + count
    return out


def as_column(row):
    n = row.shape[1]
    square = (n, n)
    here = lax.broadcasted_iota(jnp.int32, square, 0) == lax.broadcasted_iota(jnp.int32, square, 1)
    return jnp.sum(jnp.where(here, jnp.broadcast_to(row, square), 0.0), axis=1, keepdims=True)


def mask_kernel(coef_ref, limits_ref, weight_ref, send_ref, keep_ref):
    rows, width = coef_ref.shape
    tiles = width // N // AUX_PAD
    core = lax.axis_index("c")
    device = ((lax.axis_index("y") * N + lax.axis_index("x")) * N + lax.axis_index("z")) * 2 + core
    block = device * rows // PAIR_ROWS
    lane = lax.broadcasted_iota(jnp.int32, (rows, AUX_PAD), 1)
    at_block = lax.broadcasted_iota(jnp.int32, limits_ref.shape, 1) == block
    limits = jnp.sum(jnp.where(at_block, limits_ref[...], 0), axis=1, keepdims=True)
    limits = jnp.broadcast_to(limits, limits_ref.shape)
    weight = jnp.broadcast_to(as_column(weight_ref[...]), (rows, AUX_PAD))

    def store(ref, to, found):
        for t in range(tiles):
            ref[to, 0:rows, t * AUX_PAD : (t + 1) * AUX_PAD] = found[t].astype(jnp.bfloat16)

    def run(left_ref, right_ref):
        for to in range(N):
            masked = []
            for atom in range(to * tiles, (to + 1) * tiles):
                coef = coef_ref[:, atom * AUX_PAD : (atom + 1) * AUX_PAD].astype(jnp.float32)
                masked.append(jnp.where(lane < limits[atom : atom + 1, :], coef, 0.0))
            store(left_ref, to, into_order(masked))
            store(right_ref, to, [weight * m for m in masked])

    @pl.when(core == 0)
    def _():
        run(keep_ref, send_ref)

    @pl.when(core == 1)
    def _():
        run(send_ref, keep_ref)


def operands(coefficients, row_weight, pattern, aux_sizes):
    rows, width = coefficients.shape
    limits = pattern.T * aux_sizes[:, None]
    return pl.pallas_call(
        mask_kernel,
        out_shape=[jax.ShapeDtypeStruct((N, height, width // N), jnp.bfloat16) for height in (rows, 2 * rows)],
        in_specs=[VMEM] * 3,
        out_specs=[VMEM] * 2,
        compiler_params=SMALL,
        cost_estimate=pl.CostEstimate(flops=8 * rows * width, bytes_accessed=6 * rows * width, transcendentals=0),
    )(coefficients, limits, row_weight.reshape(1, -1))


def contract_part(own_refs, other_ref, gathered, part, write):
    places, two, rows, wide = own_refs[0].shape[1:]
    core = lax.axis_index("c")
    mine = jnp.where(core == 0, lax.axis_index("z"), lax.axis_index("y"))
    theirs = jnp.where(core == 0, lax.axis_index("y"), lax.axis_index("z"))
    tile = 256

    def gather(columns):
        for k, distance in enumerate(ORDER[slice(*PARTS[part])]):
            inner = lax.rem(theirs + N - distance, N)
            for own_ref, (first, last) in zip(own_refs, PARTS):
                for slot in range(first, last):
                    place = lax.rem(mine + N - ORDER[slot], N)
                    for h in range(two):
                        at = pl.multiple_of(((k * places + place) * two + h) * rows, rows)
                        gathered[pl.ds(at, rows), columns] = own_ref[slot - first, inner, 1 - h, :, columns]

    depth = other_ref.shape[0]

    def run(left_ref, right_ref, columns):
        def column_tile(t, carry):
            start = pl.multiple_of(t * tile, tile)
            write(
                start,
                lax.dot_general(
                    left_ref[0:depth, columns],
                    right_ref[0:depth, pl.ds(start, tile)],
                    (((0,), (0,)), ((), ())),
                    preferred_element_type=jnp.float32,
                ),
            )
            return carry

        lax.fori_loop(0, wide // tile, column_tile, 0)

    @pl.when(core == 0)
    def _():
        gather(slice(0, HALF))
        run(gathered, other_ref, slice(0, HALF))

    @pl.when(core == 1)
    def _():
        gather(slice(0, wide))
        run(other_ref, gathered, slice(HALF, 2 * HALF))


def contract_parts(parts, own_refs, other_refs, sum_ref, out_ref, gathered):
    for part, other_ref in zip(parts, other_refs):

        def write(start, value, before=sum_ref):
            columns = pl.ds(start, value.shape[1])
            out_ref[:, columns] = value if before is None else before[:, columns] + value

        contract_part(own_refs, other_ref, gathered, part, write)
        sum_ref = out_ref


def first_parts_kernel(parts, *refs):
    own, other, (out_ref, gathered) = refs[: len(PARTS)], refs[len(PARTS) : -2], refs[-2:]
    contract_parts(parts, own, other, None, out_ref, gathered)


def last_part_kernel(parts, *refs):
    own, other, (first_ref, out_ref, gathered, total) = refs[: len(PARTS)], refs[len(PARTS) : -4], refs[-4:]
    contract_parts(parts, own, other, first_ref, total, gathered)

    lanes = out_ref.shape[2]
    tiles = total.shape[1] // lanes
    tail = out_ref.shape[1] - tiles * ROWS
    at_row = lax.broadcasted_iota(jnp.int32, (tail, lanes), 0)

    def message(d, carry):
        rows = pl.ds(pl.multiple_of(d * ROWS, 16), ROWS)
        exponents = jnp.zeros((tail, lanes), jnp.int32)
        for t in range(tiles):
            value = total[rows, t * lanes : (t + 1) * lanes]
            largest = jnp.max(jnp.abs(value), axis=0, keepdims=True)
            exponent = jnp.floor(jnp.log2(jnp.maximum(largest, 2.0**-110)))
            coded = jnp.floor(value * jnp.exp2(STEPS - exponent) + 0.5)
            coded = jnp.clip(coded, -32767.0, 32767.0).astype(jnp.int32)
            out_ref[d, t * ROWS : (t + 1) * ROWS, :] = coded.astype(jnp.int16)
            exponents = jnp.where(at_row == t, exponent.astype(jnp.int32), exponents)
        out_ref[d, tiles * ROWS :, :] = exponents.astype(jnp.int16)
        return carry

    lax.fori_loop(0, out_ref.shape[0], message, 0)


def sum_kernel(parts_ref, out_ref):
    messages, _, lanes = parts_ref.shape
    tiles = out_ref.shape[1] // lanes
    scales = [
        jnp.exp2(parts_ref[d, tiles * ROWS :, :].astype(jnp.int32).astype(jnp.float32) - STEPS) for d in range(messages)
    ]
    for t in range(tiles):
        total = jnp.zeros((ROWS, lanes), jnp.float32)
        for d in range(messages):
            coded = parts_ref[d, t * ROWS : (t + 1) * ROWS, :].astype(jnp.int32)
            total = total + coded.astype(jnp.float32) * scales[d][t : t + 1, :]
        out_ref[:, t * lanes : (t + 1) * lanes] = total


def contract(own, other):
    wide = own[0].shape[-1]
    *early, last = range(len(PARTS))
    depths = [o.shape[0] for o in other]
    gathered = lambda parts: pltpu.VMEM((max(depths[p] for p in parts), wide), jnp.bfloat16)
    cost = lambda parts: pl.CostEstimate(
        flops=2 * sum(depths[p] for p in parts) * wide * HALF,
        bytes_accessed=8 * sum(depths[p] for p in parts) * wide,
        transcendentals=0,
    )
    params = pltpu.CompilerParams(vmem_limit_bytes=32 * 2**20)
    first = pl.pallas_call(
        functools.partial(first_parts_kernel, early),
        out_shape=jax.ShapeDtypeStruct((HALF, wide), jnp.float32),
        in_specs=[VMEM] * (len(PARTS) + len(early)),
        out_specs=VMEM,
        scratch_shapes=[gathered(early)],
        compiler_params=params,
        cost_estimate=cost(early),
    )(*own, *[other[p] for p in early])
    lanes = 128
    return pl.pallas_call(
        functools.partial(last_part_kernel, [last]),
        out_shape=jax.ShapeDtypeStruct((HALF // ROWS, wide // lanes * ROWS + 16, lanes), jnp.int16),
        in_specs=[VMEM] * (len(PARTS) + 2),
        out_specs=VMEM,
        scratch_shapes=[gathered([last]), pltpu.VMEM((HALF, wide), jnp.float32)],
        compiler_params=params,
        cost_estimate=cost([last]),
    )(*own, other[last], first)


def along(first, second, distance):
    pairs = []
    for ring in groups(first, second):
        pairs += [(ring[i], ring[(i + distance) % N]) for i in range(N)]
    return pairs


def per_device(coefficients, row_weight, pattern, aux_sizes):
    rows = coefficients.shape[0]
    swap = [(0, 1), (1, 0)]
    send, keep = operands(coefficients, row_weight, pattern, aux_sizes)
    blocks = lax.dynamic_update_slice(keep, lax.ppermute(send, "c", swap), (0, rows, 0))
    wide = blocks.shape[2]
    blocks = exchange(blocks, "y", "z").reshape(N, 2, rows, wide)
    move = lambda value, d: lax.ppermute(value, AXES, along("z", "y", d))
    slot = {0: blocks, 2: move(blocks, 2), 6: move(blocks, -2), 1: move(blocks, 1), 7: move(blocks, -1)}
    slot[3], slot[5] = move(slot[2], 1), move(slot[6], -1)
    slot[4] = jnp.concatenate([move(slot[2][: N // 2], 2), move(slot[6][N // 2 :], -2)])
    own = [jnp.stack([slot[d] for d in ORDER[slice(*part)]]) for part in PARTS]
    other = [lax.ppermute(part, "c", swap).reshape(-1, wide) for part in own]
    messages = contract(own, other)
    parts = lax.all_to_all(messages, "x", 0, 0, tiled=True)
    return pl.pallas_call(
        sum_kernel,
        out_shape=jax.ShapeDtypeStruct((ROWS, wide), jnp.float32),
        in_specs=[VMEM],
        out_specs=VMEM,
        compiler_params=SMALL,
    )(parts)


def solution(mesh):
    grid = Mesh(mesh.devices.reshape(N, N, N, 2), AXES)
    placed = (P(AXES, None), P(AXES), P(), P())
    return jax.shard_map(
        per_device,
        mesh=grid,
        in_specs=placed,
        out_specs=P(("y", "x", "c"), "z"),
        check_vma=False,
    )
```

```python
import functools
import itertools

import jax
import jax.numpy as jnp
from jax import lax
from jax.experimental import pallas as pl
from jax.experimental.pallas import tpu as pltpu
from jax.sharding import Mesh, PartitionSpec as P

PAIR_ROWS = 128
AUX_PAD = 128
N = 8
AXES = ("y", "x", "z", "c")
HALF = 384
ROWS = 48
OFFSETS = (0, -2, 2, 1, -1, 3, -3, 4)
PARTS = ((0, 4), (4, 8))
STEPS = 14
VMEM = pl.BlockSpec(memory_space=pltpu.VMEM)
SMALL = pltpu.CompilerParams(vmem_limit_bytes=8 * 2**20)


def groups(first, second):
    found = []
    for core, axis in enumerate((first, second)):
        rest = [a for a in "yxz" if a != axis]
        for others in itertools.product(range(N), repeat=2):
            at = dict(zip(rest, others))
            ring = []
            for i in range(N):
                at[axis] = i
                ring.append(((at["y"] * N + at["x"]) * N + at["z"]) * 2 + core)
            found.append(ring)
    return found


def exchange(blocks, first, second):
    return lax.all_to_all(
        blocks, AXES, 0, 0, tiled=True, axis_index_groups=groups(first, second)
    )


def into_order(tiles):
    lanes = tiles[0].shape[1]
    lane = lax.broadcasted_iota(jnp.int32, tiles[0].shape, 1)
    out = [None] * len(tiles)
    for piece in range(2 * N):
        core, x = divmod(piece, N)
        to, source = piece * ROWS, (2 * x + core) * ROWS
        end = to + ROWS
        while to < end:
            count = min(end - to, lanes - to % lanes, lanes - source % lanes)
            tile, start = divmod(to, lanes)
            rolled = tiles[source // lanes]
            if (to - source) % lanes:
                rolled = pltpu.roll(rolled, (to - source) % lanes, 1)
            out[tile] = rolled if start == 0 else jnp.where(lane >= start, rolled, out[tile])
            to, source = to + count, source + count
    return out


def as_column(row):
    n = row.shape[1]
    square = (n, n)
    here = lax.broadcasted_iota(jnp.int32, square, 0) == lax.broadcasted_iota(jnp.int32, square, 1)
    return jnp.sum(jnp.where(here, jnp.broadcast_to(row, square), 0.0), axis=1, keepdims=True)


def mask_kernel(coef_ref, limits_ref, weight_ref, send_ref, keep_ref):
    rows, width = coef_ref.shape
    tiles = width // N // AUX_PAD
    core = lax.axis_index("c")
    device = ((lax.axis_index("y") * N + lax.axis_index("x")) * N + lax.axis_index("z")) * 2 + core
    block = device * rows // PAIR_ROWS
    lane = lax.broadcasted_iota(jnp.int32, (rows, AUX_PAD), 1)
    at_block = lax.broadcasted_iota(jnp.int32, limits_ref.shape, 1) == block
    limits = jnp.sum(jnp.where(at_block, limits_ref[...], 0), axis=1, keepdims=True)
    limits = jnp.broadcast_to(limits, limits_ref.shape)
    weight = jnp.broadcast_to(as_column(weight_ref[...]), (rows, AUX_PAD))

    def store(ref, to, found):
        for t in range(tiles):
            ref[to, 0:rows, t * AUX_PAD : (t + 1) * AUX_PAD] = found[t].astype(jnp.bfloat16)

    def run(left_ref, right_ref):
        for to in range(N):
            masked = []
            for atom in range(to * tiles, (to + 1) * tiles):
                coef = coef_ref[:, atom * AUX_PAD : (atom + 1) * AUX_PAD].astype(jnp.float32)
                masked.append(jnp.where(lane < limits[atom : atom + 1, :], coef, 0.0))
            store(left_ref, to, into_order(masked))
            store(right_ref, to, [weight * m for m in masked])

    @pl.when(core == 0)
    def _():
        run(keep_ref, send_ref)

    @pl.when(core == 1)
    def _():
        run(send_ref, keep_ref)


def operands(coefficients, row_weight, pattern, aux_sizes):
    rows, width = coefficients.shape
    limits = pattern.T * aux_sizes[:, None]
    return pl.pallas_call(
        mask_kernel,
        out_shape=[jax.ShapeDtypeStruct((N, height, width // N), jnp.bfloat16) for height in (rows, 2 * rows)],
        in_specs=[VMEM] * 3,
        out_specs=[VMEM] * 2,
        compiler_params=SMALL,
        cost_estimate=pl.CostEstimate(flops=8 * rows * width, bytes_accessed=6 * rows * width, transcendentals=0),
    )(coefficients, limits, row_weight.reshape(1, -1))


def away(place, offset):
    return lax.rem(place + (1 - 2 * lax.rem(place, 2)) * offset + N, N)


def contract_part(own_refs, other_ref, gathered, part, write):
    places, two, rows, wide = own_refs[0].shape[1:]
    core = lax.axis_index("c")
    mine = jnp.where(core == 0, lax.axis_index("z"), lax.axis_index("y"))
    theirs = jnp.where(core == 0, lax.axis_index("y"), lax.axis_index("z"))
    tile = 256

    def gather(columns):
        for k, offset in enumerate(OFFSETS[slice(*PARTS[part])]):
            inner = away(theirs, offset)
            for own_ref, (first, last) in zip(own_refs, PARTS):
                for slot in range(first, last):
                    place = away(mine, OFFSETS[slot])
                    for h in range(two):
                        at = pl.multiple_of(((k * places + place) * two + h) * rows, rows)
                        gathered[pl.ds(at, rows), columns] = own_ref[slot - first, inner, 1 - h, :, columns]

    depth = other_ref.shape[0]

    def run(left_ref, right_ref, columns):
        def column_tile(t, carry):
            start = pl.multiple_of(t * tile, tile)
            write(
                start,
                lax.dot_general(
                    left_ref[0:depth, columns],
                    right_ref[0:depth, pl.ds(start, tile)],
                    (((0,), (0,)), ((), ())),
                    preferred_element_type=jnp.float32,
                ),
            )
            return carry

        lax.fori_loop(0, wide // tile, column_tile, 0)

    @pl.when(core == 0)
    def _():
        gather(slice(0, HALF))
        run(gathered, other_ref, slice(0, HALF))

    @pl.when(core == 1)
    def _():
        gather(slice(0, wide))
        run(other_ref, gathered, slice(HALF, 2 * HALF))


def contract_parts(parts, own_refs, other_refs, sum_ref, out_ref, gathered):
    for part, other_ref in zip(parts, other_refs):

        def write(start, value, before=sum_ref):
            columns = pl.ds(start, value.shape[1])
            out_ref[:, columns] = value if before is None else before[:, columns] + value

        contract_part(own_refs, other_ref, gathered, part, write)
        sum_ref = out_ref


def first_parts_kernel(parts, *refs):
    own, other, (out_ref, gathered) = refs[: len(PARTS)], refs[len(PARTS) : -2], refs[-2:]
    contract_parts(parts, own, other, None, out_ref, gathered)


def last_part_kernel(parts, *refs):
    own, other, (first_ref, out_ref, gathered, total) = refs[: len(PARTS)], refs[len(PARTS) : -4], refs[-4:]
    contract_parts(parts, own, other, first_ref, total, gathered)

    lanes = out_ref.shape[2]
    tiles = total.shape[1] // lanes
    tail = out_ref.shape[1] - tiles * ROWS
    at_row = lax.broadcasted_iota(jnp.int32, (tail, lanes), 0)

    def message(d, carry):
        rows = pl.ds(pl.multiple_of(d * ROWS, 16), ROWS)
        exponents = jnp.zeros((tail, lanes), jnp.int32)
        for t in range(tiles):
            value = total[rows, t * lanes : (t + 1) * lanes]
            largest = jnp.max(jnp.abs(value), axis=0, keepdims=True)
            exponent = jnp.floor(jnp.log2(jnp.maximum(largest, 2.0**-110)))
            coded = jnp.floor(value * jnp.exp2(STEPS - exponent) + 0.5)
            coded = jnp.clip(coded, -32767.0, 32767.0).astype(jnp.int32)
            out_ref[d, t * ROWS : (t + 1) * ROWS, :] = coded.astype(jnp.int16)
            exponents = jnp.where(at_row == t, exponent.astype(jnp.int32), exponents)
        out_ref[d, tiles * ROWS :, :] = exponents.astype(jnp.int16)
        return carry

    lax.fori_loop(0, out_ref.shape[0], message, 0)


def sum_kernel(parts_ref, out_ref):
    messages, _, lanes = parts_ref.shape
    tiles = out_ref.shape[1] // lanes
    scales = [
        jnp.exp2(parts_ref[d, tiles * ROWS :, :].astype(jnp.int32).astype(jnp.float32) - STEPS) for d in range(messages)
    ]
    for t in range(tiles):
        total = jnp.zeros((ROWS, lanes), jnp.float32)
        for d in range(messages):
            coded = parts_ref[d, t * ROWS : (t + 1) * ROWS, :].astype(jnp.int32)
            total = total + coded.astype(jnp.float32) * scales[d][t : t + 1, :]
        out_ref[:, t * lanes : (t + 1) * lanes] = total


def contract(own, other):
    wide = own[0].shape[-1]
    *early, last = range(len(PARTS))
    depths = [o.shape[0] for o in other]
    gathered = lambda parts: pltpu.VMEM((max(depths[p] for p in parts), wide), jnp.bfloat16)
    cost = lambda parts: pl.CostEstimate(
        flops=2 * sum(depths[p] for p in parts) * wide * HALF,
        bytes_accessed=8 * sum(depths[p] for p in parts) * wide,
        transcendentals=0,
    )
    params = pltpu.CompilerParams(vmem_limit_bytes=32 * 2**20)
    first = pl.pallas_call(
        functools.partial(first_parts_kernel, early),
        out_shape=jax.ShapeDtypeStruct((HALF, wide), jnp.float32),
        in_specs=[VMEM] * (len(PARTS) + len(early)),
        out_specs=VMEM,
        scratch_shapes=[gathered(early)],
        compiler_params=params,
        cost_estimate=cost(early),
    )(*own, *[other[p] for p in early])
    lanes = 128
    return pl.pallas_call(
        functools.partial(last_part_kernel, [last]),
        out_shape=jax.ShapeDtypeStruct((HALF // ROWS, wide // lanes * ROWS + 16, lanes), jnp.int16),
        in_specs=[VMEM] * (len(PARTS) + 2),
        out_specs=VMEM,
        scratch_shapes=[gathered([last]), pltpu.VMEM((HALF, wide), jnp.float32)],
        compiler_params=params,
        cost_estimate=cost([last]),
    )(*own, other[last], first)


def along(first, second, step):
    pairs = []
    for ring in groups(first, second):
        pairs += [(ring[i], ring[(i + (step if i % 2 == 0 else -step)) % N]) for i in range(N)]
    return pairs


def per_device(coefficients, row_weight, pattern, aux_sizes):
    rows = coefficients.shape[0]
    swap = [(0, 1), (1, 0)]
    send, keep = operands(coefficients, row_weight, pattern, aux_sizes)
    blocks = lax.dynamic_update_slice(keep, lax.ppermute(send, "c", swap), (0, rows, 0))
    wide = blocks.shape[2]
    blocks = exchange(blocks, "y", "z").reshape(N, 2, rows, wide)
    move = lambda value, step: lax.ppermute(value, AXES, along("z", "y", step))
    slot = {0: blocks, -2: move(blocks, 2), 2: move(blocks, -2), 1: move(blocks, 1), -1: move(blocks, -1)}
    slot[4], slot[3], slot[-3] = move(slot[-2], 2), move(slot[-2], 1), move(slot[2], -1)
    own = [jnp.stack([slot[k] for k in OFFSETS[slice(*part)]]) for part in PARTS]
    other = [lax.ppermute(part, "c", swap).reshape(-1, wide) for part in own]
    messages = contract(own, other)
    parts = lax.all_to_all(messages, "x", 0, 0, tiled=True)
    return pl.pallas_call(
        sum_kernel,
        out_shape=jax.ShapeDtypeStruct((ROWS, wide), jnp.float32),
        in_specs=[VMEM],
        out_specs=VMEM,
        compiler_params=SMALL,
    )(parts)


def solution(mesh):
    grid = Mesh(mesh.devices.reshape(N, N, N, 2), AXES)
    placed = (P(AXES, None), P(AXES), P(), P())
    return jax.shard_map(
        per_device,
        mesh=grid,
        in_specs=placed,
        out_specs=P(("y", "x", "c"), "z"),
        check_vma=False,
    )
```

```python
import functools
import itertools

import jax
import jax.numpy as jnp
from jax import lax
from jax.experimental import pallas as pl
from jax.experimental.pallas import tpu as pltpu
from jax.sharding import Mesh, PartitionSpec as P

PAIR_ROWS = 128
AUX_PAD = 128
N = 8
AXES = ("y", "x", "z", "c")
HALF = 384
ROWS = 48
OFFSETS = (0, -2, 2, 4, 1, -1, 3, -3)
PARTS = ((0, 4), (4, 8))
STEPS = 14
VMEM = pl.BlockSpec(memory_space=pltpu.VMEM)
SMALL = pltpu.CompilerParams(vmem_limit_bytes=8 * 2**20)


def groups(first, second):
    found = []
    for core, axis in enumerate((first, second)):
        rest = [a for a in "yxz" if a != axis]
        for others in itertools.product(range(N), repeat=2):
            at = dict(zip(rest, others))
            ring = []
            for i in range(N):
                at[axis] = i
                ring.append(((at["y"] * N + at["x"]) * N + at["z"]) * 2 + core)
            found.append(ring)
    return found


def exchange(blocks, first, second):
    return lax.all_to_all(
        blocks, AXES, 0, 0, tiled=True, axis_index_groups=groups(first, second)
    )


def into_order(tiles):
    lanes = tiles[0].shape[1]
    lane = lax.broadcasted_iota(jnp.int32, tiles[0].shape, 1)
    out = [None] * len(tiles)
    for piece in range(2 * N):
        core, x = divmod(piece, N)
        to, source = piece * ROWS, (2 * x + core) * ROWS
        end = to + ROWS
        while to < end:
            count = min(end - to, lanes - to % lanes, lanes - source % lanes)
            tile, start = divmod(to, lanes)
            rolled = tiles[source // lanes]
            if (to - source) % lanes:
                rolled = pltpu.roll(rolled, (to - source) % lanes, 1)
            out[tile] = rolled if start == 0 else jnp.where(lane >= start, rolled, out[tile])
            to, source = to + count, source + count
    return out


def as_column(row):
    n = row.shape[1]
    square = (n, n)
    here = lax.broadcasted_iota(jnp.int32, square, 0) == lax.broadcasted_iota(jnp.int32, square, 1)
    return jnp.sum(jnp.where(here, jnp.broadcast_to(row, square), 0.0), axis=1, keepdims=True)


def mask_kernel(coef_ref, limits_ref, weight_ref, send_ref, keep_ref):
    rows, width = coef_ref.shape
    tiles = width // N // AUX_PAD
    core = lax.axis_index("c")
    device = ((lax.axis_index("y") * N + lax.axis_index("x")) * N + lax.axis_index("z")) * 2 + core
    block = device * rows // PAIR_ROWS
    lane = lax.broadcasted_iota(jnp.int32, (rows, AUX_PAD), 1)
    at_block = lax.broadcasted_iota(jnp.int32, limits_ref.shape, 1) == block
    limits = jnp.sum(jnp.where(at_block, limits_ref[...], 0), axis=1, keepdims=True)
    limits = jnp.broadcast_to(limits, limits_ref.shape)
    weight = jnp.broadcast_to(as_column(weight_ref[...]), (rows, AUX_PAD))

    def store(ref, to, found):
        for t in range(tiles):
            ref[to, 0:rows, t * AUX_PAD : (t + 1) * AUX_PAD] = found[t].astype(jnp.bfloat16)

    def run(left_ref, right_ref):
        for to in range(N):
            masked = []
            for atom in range(to * tiles, (to + 1) * tiles):
                coef = coef_ref[:, atom * AUX_PAD : (atom + 1) * AUX_PAD].astype(jnp.float32)
                masked.append(jnp.where(lane < limits[atom : atom + 1, :], coef, 0.0))
            store(left_ref, to, into_order(masked))
            store(right_ref, to, [weight * m for m in masked])

    @pl.when(core == 0)
    def _():
        run(keep_ref, send_ref)

    @pl.when(core == 1)
    def _():
        run(send_ref, keep_ref)


def operands(coefficients, row_weight, pattern, aux_sizes):
    rows, width = coefficients.shape
    limits = pattern.T * aux_sizes[:, None]
    return pl.pallas_call(
        mask_kernel,
        out_shape=[jax.ShapeDtypeStruct((N, height, width // N), jnp.bfloat16) for height in (rows, 2 * rows)],
        in_specs=[VMEM] * 3,
        out_specs=[VMEM] * 2,
        compiler_params=SMALL,
        cost_estimate=pl.CostEstimate(flops=8 * rows * width, bytes_accessed=6 * rows * width, transcendentals=0),
    )(coefficients, limits, row_weight.reshape(1, -1))


def away(place, offset):
    return lax.rem(place + (1 - 2 * lax.rem(place, 2)) * offset + N, N)


def contract_part(own_refs, other_ref, gathered, part, write):
    places, two, rows, wide = own_refs[0].shape[1:]
    core = lax.axis_index("c")
    mine = jnp.where(core == 0, lax.axis_index("z"), lax.axis_index("y"))
    theirs = jnp.where(core == 0, lax.axis_index("y"), lax.axis_index("z"))
    tile = 256

    def gather(columns):
        for k, offset in enumerate(OFFSETS[slice(*PARTS[part])]):
            inner = away(theirs, offset)
            for own_ref, (first, last) in zip(own_refs, PARTS):
                for slot in range(first, last):
                    place = away(mine, OFFSETS[slot])
                    for h in range(two):
                        at = pl.multiple_of(((k * places + place) * two + h) * rows, rows)
                        gathered[pl.ds(at, rows), columns] = own_ref[slot - first, inner, 1 - h, :, columns]

    depth = other_ref.shape[0]

    def run(left_ref, right_ref, columns):
        def column_tile(t, carry):
            start = pl.multiple_of(t * tile, tile)
            write(
                start,
                lax.dot_general(
                    left_ref[0:depth, columns],
                    right_ref[0:depth, pl.ds(start, tile)],
                    (((0,), (0,)), ((), ())),
                    preferred_element_type=jnp.float32,
                ),
            )
            return carry

        lax.fori_loop(0, wide // tile, column_tile, 0)

    @pl.when(core == 0)
    def _():
        gather(slice(0, HALF))
        run(gathered, other_ref, slice(0, HALF))

    @pl.when(core == 1)
    def _():
        gather(slice(0, wide))
        run(other_ref, gathered, slice(HALF, 2 * HALF))


def contract_parts(parts, own_refs, other_refs, sum_ref, out_ref, gathered):
    for part, other_ref in zip(parts, other_refs):

        def write(start, value, before=sum_ref):
            columns = pl.ds(start, value.shape[1])
            out_ref[:, columns] = value if before is None else before[:, columns] + value

        contract_part(own_refs, other_ref, gathered, part, write)
        sum_ref = out_ref


def first_parts_kernel(parts, *refs):
    own, other, (out_ref, gathered) = refs[: len(PARTS)], refs[len(PARTS) : -2], refs[-2:]
    contract_parts(parts, own, other, None, out_ref, gathered)


def last_part_kernel(parts, *refs):
    own, other, (first_ref, out_ref, gathered, total) = refs[: len(PARTS)], refs[len(PARTS) : -4], refs[-4:]
    contract_parts(parts, own, other, first_ref, total, gathered)

    lanes = out_ref.shape[2]
    tiles = total.shape[1] // lanes
    tail = out_ref.shape[1] - tiles * ROWS
    at_row = lax.broadcasted_iota(jnp.int32, (tail, lanes), 0)

    def message(d, carry):
        rows = pl.ds(pl.multiple_of(d * ROWS, 16), ROWS)
        exponents = jnp.zeros((tail, lanes), jnp.int32)
        for t in range(tiles):
            value = total[rows, t * lanes : (t + 1) * lanes]
            largest = jnp.max(jnp.abs(value), axis=0, keepdims=True)
            exponent = jnp.floor(jnp.log2(jnp.maximum(largest, 2.0**-110)))
            coded = jnp.floor(value * jnp.exp2(STEPS - exponent) + 0.5)
            coded = jnp.clip(coded, -32767.0, 32767.0).astype(jnp.int32)
            out_ref[d, t * ROWS : (t + 1) * ROWS, :] = coded.astype(jnp.int16)
            exponents = jnp.where(at_row == t, exponent.astype(jnp.int32), exponents)
        out_ref[d, tiles * ROWS :, :] = exponents.astype(jnp.int16)
        return carry

    lax.fori_loop(0, out_ref.shape[0], message, 0)


def sum_kernel(parts_ref, out_ref):
    messages, _, lanes = parts_ref.shape
    tiles = out_ref.shape[1] // lanes
    scales = [
        jnp.exp2(parts_ref[d, tiles * ROWS :, :].astype(jnp.int32).astype(jnp.float32) - STEPS) for d in range(messages)
    ]
    for t in range(tiles):
        total = jnp.zeros((ROWS, lanes), jnp.float32)
        for d in range(messages):
            coded = parts_ref[d, t * ROWS : (t + 1) * ROWS, :].astype(jnp.int32)
            total = total + coded.astype(jnp.float32) * scales[d][t : t + 1, :]
        out_ref[:, t * lanes : (t + 1) * lanes] = total


def contract(own, other):
    wide = own[0].shape[-1]
    *early, last = range(len(PARTS))
    depths = [o.shape[0] for o in other]
    gathered = lambda parts: pltpu.VMEM((max(depths[p] for p in parts), wide), jnp.bfloat16)
    cost = lambda parts: pl.CostEstimate(
        flops=2 * sum(depths[p] for p in parts) * wide * HALF,
        bytes_accessed=8 * sum(depths[p] for p in parts) * wide,
        transcendentals=0,
    )
    params = pltpu.CompilerParams(vmem_limit_bytes=32 * 2**20)
    first = pl.pallas_call(
        functools.partial(first_parts_kernel, early),
        out_shape=jax.ShapeDtypeStruct((HALF, wide), jnp.float32),
        in_specs=[VMEM] * (len(PARTS) + len(early)),
        out_specs=VMEM,
        scratch_shapes=[gathered(early)],
        compiler_params=params,
        cost_estimate=cost(early),
    )(*own, *[other[p] for p in early])
    lanes = 128
    return pl.pallas_call(
        functools.partial(last_part_kernel, [last]),
        out_shape=jax.ShapeDtypeStruct((HALF // ROWS, wide // lanes * ROWS + 16, lanes), jnp.int16),
        in_specs=[VMEM] * (len(PARTS) + 2),
        out_specs=VMEM,
        scratch_shapes=[gathered([last]), pltpu.VMEM((HALF, wide), jnp.float32)],
        compiler_params=params,
        cost_estimate=cost([last]),
    )(*own, other[last], first)


def along(first, second, step):
    pairs = []
    for ring in groups(first, second):
        pairs += [(ring[i], ring[(i + (step if i % 2 == 0 else -step)) % N]) for i in range(N)]
    return pairs


def per_device(coefficients, row_weight, pattern, aux_sizes):
    rows = coefficients.shape[0]
    swap = [(0, 1), (1, 0)]
    send, keep = operands(coefficients, row_weight, pattern, aux_sizes)
    blocks = lax.dynamic_update_slice(keep, lax.ppermute(send, "c", swap), (0, rows, 0))
    wide = blocks.shape[2]
    blocks = exchange(blocks, "y", "z").reshape(N, 2, rows, wide)
    move = lambda value, step: lax.ppermute(value, AXES, along("z", "y", step))
    slot = {0: blocks, -2: move(blocks, 2), 2: move(blocks, -2), 1: move(blocks, 1), -1: move(blocks, -1)}
    slot[4], slot[3], slot[-3] = move(slot[-2], 2), move(slot[-2], 1), move(slot[2], -1)
    own = [jnp.stack([slot[k] for k in OFFSETS[slice(*part)]]) for part in PARTS]
    other = [lax.ppermute(part, "c", swap).reshape(-1, wide) for part in own]
    messages = contract(own, other)
    parts = lax.all_to_all(messages, "x", 0, 0, tiled=True)
    return pl.pallas_call(
        sum_kernel,
        out_shape=jax.ShapeDtypeStruct((ROWS, wide), jnp.float32),
        in_specs=[VMEM],
        out_specs=VMEM,
        compiler_params=SMALL,
    )(parts)


def solution(mesh):
    grid = Mesh(mesh.devices.reshape(N, N, N, 2), AXES)
    placed = (P(AXES, None), P(AXES), P(), P())
    return jax.shard_map(
        per_device,
        mesh=grid,
        in_specs=placed,
        out_specs=P(("y", "x", "c"), "z"),
        check_vma=False,
    )
```

```python
import functools
import itertools

import jax
import jax.numpy as jnp
from jax import lax
from jax.experimental import pallas as pl
from jax.experimental.pallas import tpu as pltpu
from jax.sharding import Mesh, PartitionSpec as P

PAIR_ROWS = 128
AUX_PAD = 128
N = 8
AXES = ("y", "x", "z", "c")
HALF = 384
ROWS = 48
OFFSETS = (0, -2, 1, -1, 2, 3, -3, 4)
PARTS = ((0, 4), (4, 8))
STEPS = 14
VMEM = pl.BlockSpec(memory_space=pltpu.VMEM)
SMALL = pltpu.CompilerParams(vmem_limit_bytes=8 * 2**20)


def groups(first, second):
    found = []
    for core, axis in enumerate((first, second)):
        rest = [a for a in "yxz" if a != axis]
        for others in itertools.product(range(N), repeat=2):
            at = dict(zip(rest, others))
            ring = []
            for i in range(N):
                at[axis] = i
                ring.append(((at["y"] * N + at["x"]) * N + at["z"]) * 2 + core)
            found.append(ring)
    return found


def exchange(blocks, first, second):
    return lax.all_to_all(
        blocks, AXES, 0, 0, tiled=True, axis_index_groups=groups(first, second)
    )


def into_order(tiles):
    lanes = tiles[0].shape[1]
    lane = lax.broadcasted_iota(jnp.int32, tiles[0].shape, 1)
    out = [None] * len(tiles)
    for piece in range(2 * N):
        core, x = divmod(piece, N)
        to, source = piece * ROWS, (2 * x + core) * ROWS
        end = to + ROWS
        while to < end:
            count = min(end - to, lanes - to % lanes, lanes - source % lanes)
            tile, start = divmod(to, lanes)
            rolled = tiles[source // lanes]
            if (to - source) % lanes:
                rolled = pltpu.roll(rolled, (to - source) % lanes, 1)
            out[tile] = rolled if start == 0 else jnp.where(lane >= start, rolled, out[tile])
            to, source = to + count, source + count
    return out


def as_column(row):
    n = row.shape[1]
    square = (n, n)
    here = lax.broadcasted_iota(jnp.int32, square, 0) == lax.broadcasted_iota(jnp.int32, square, 1)
    return jnp.sum(jnp.where(here, jnp.broadcast_to(row, square), 0.0), axis=1, keepdims=True)


def mask_kernel(coef_ref, limits_ref, weight_ref, send_ref, keep_ref):
    rows, width = coef_ref.shape
    tiles = width // N // AUX_PAD
    core = lax.axis_index("c")
    device = ((lax.axis_index("y") * N + lax.axis_index("x")) * N + lax.axis_index("z")) * 2 + core
    block = device * rows // PAIR_ROWS
    lane = lax.broadcasted_iota(jnp.int32, (rows, AUX_PAD), 1)
    at_block = lax.broadcasted_iota(jnp.int32, limits_ref.shape, 1) == block
    limits = jnp.sum(jnp.where(at_block, limits_ref[...], 0), axis=1, keepdims=True)
    limits = jnp.broadcast_to(limits, limits_ref.shape)
    weight = jnp.broadcast_to(as_column(weight_ref[...]), (rows, AUX_PAD))

    def store(ref, to, found):
        for t in range(tiles):
            ref[to, 0:rows, t * AUX_PAD : (t + 1) * AUX_PAD] = found[t].astype(jnp.bfloat16)

    def run(left_ref, right_ref):
        for to in range(N):
            masked = []
            for atom in range(to * tiles, (to + 1) * tiles):
                coef = coef_ref[:, atom * AUX_PAD : (atom + 1) * AUX_PAD].astype(jnp.float32)
                masked.append(jnp.where(lane < limits[atom : atom + 1, :], coef, 0.0))
            store(left_ref, to, into_order(masked))
            store(right_ref, to, [weight * m for m in masked])

    @pl.when(core == 0)
    def _():
        run(keep_ref, send_ref)

    @pl.when(core == 1)
    def _():
        run(send_ref, keep_ref)


def operands(coefficients, row_weight, pattern, aux_sizes):
    rows, width = coefficients.shape
    limits = pattern.T * aux_sizes[:, None]
    return pl.pallas_call(
        mask_kernel,
        out_shape=[jax.ShapeDtypeStruct((N, height, width // N), jnp.bfloat16) for height in (rows, 2 * rows)],
        in_specs=[VMEM] * 3,
        out_specs=[VMEM] * 2,
        compiler_params=SMALL,
        cost_estimate=pl.CostEstimate(flops=8 * rows * width, bytes_accessed=6 * rows * width, transcendentals=0),
    )(coefficients, limits, row_weight.reshape(1, -1))


def away(place, offset):
    return lax.rem(place + (1 - 2 * lax.rem(place, 2)) * offset + N, N)


def contract_part(own_refs, other_ref, gathered, part, write):
    places, two, rows, wide = own_refs[0].shape[1:]
    core = lax.axis_index("c")
    mine = jnp.where(core == 0, lax.axis_index("z"), lax.axis_index("y"))
    theirs = jnp.where(core == 0, lax.axis_index("y"), lax.axis_index("z"))
    tile = 256

    def gather(columns):
        for k, offset in enumerate(OFFSETS[slice(*PARTS[part])]):
            inner = away(theirs, offset)
            for own_ref, (first, last) in zip(own_refs, PARTS):
                for slot in range(first, last):
                    place = away(mine, OFFSETS[slot])
                    for h in range(two):
                        at = pl.multiple_of(((k * places + place) * two + h) * rows, rows)
                        gathered[pl.ds(at, rows), columns] = own_ref[slot - first, inner, 1 - h, :, columns]

    depth = other_ref.shape[0]

    def run(left_ref, right_ref, columns):
        def column_tile(t, carry):
            start = pl.multiple_of(t * tile, tile)
            write(
                start,
                lax.dot_general(
                    left_ref[0:depth, columns],
                    right_ref[0:depth, pl.ds(start, tile)],
                    (((0,), (0,)), ((), ())),
                    preferred_element_type=jnp.float32,
                ),
            )
            return carry

        lax.fori_loop(0, wide // tile, column_tile, 0)

    @pl.when(core == 0)
    def _():
        gather(slice(0, HALF))
        run(gathered, other_ref, slice(0, HALF))

    @pl.when(core == 1)
    def _():
        gather(slice(0, wide))
        run(other_ref, gathered, slice(HALF, 2 * HALF))


def contract_parts(parts, own_refs, other_refs, sum_ref, out_ref, gathered):
    for part, other_ref in zip(parts, other_refs):

        def write(start, value, before=sum_ref):
            columns = pl.ds(start, value.shape[1])
            out_ref[:, columns] = value if before is None else before[:, columns] + value

        contract_part(own_refs, other_ref, gathered, part, write)
        sum_ref = out_ref


def first_parts_kernel(parts, *refs):
    own, other, (out_ref, gathered) = refs[: len(PARTS)], refs[len(PARTS) : -2], refs[-2:]
    contract_parts(parts, own, other, None, out_ref, gathered)


def last_part_kernel(parts, *refs):
    own, other, (first_ref, out_ref, gathered, total) = refs[: len(PARTS)], refs[len(PARTS) : -4], refs[-4:]
    contract_parts(parts, own, other, first_ref, total, gathered)

    lanes = out_ref.shape[2]
    tiles = total.shape[1] // lanes
    tail = out_ref.shape[1] - tiles * ROWS
    at_row = lax.broadcasted_iota(jnp.int32, (tail, lanes), 0)

    def message(d, carry):
        rows = pl.ds(pl.multiple_of(d * ROWS, 16), ROWS)
        exponents = jnp.zeros((tail, lanes), jnp.int32)
        for t in range(tiles):
            value = total[rows, t * lanes : (t + 1) * lanes]
            largest = jnp.max(jnp.abs(value), axis=0, keepdims=True)
            exponent = jnp.floor(jnp.log2(jnp.maximum(largest, 2.0**-110)))
            coded = jnp.floor(value * jnp.exp2(STEPS - exponent) + 0.5)
            coded = jnp.clip(coded, -32767.0, 32767.0).astype(jnp.int32)
            out_ref[d, t * ROWS : (t + 1) * ROWS, :] = coded.astype(jnp.int16)
            exponents = jnp.where(at_row == t, exponent.astype(jnp.int32), exponents)
        out_ref[d, tiles * ROWS :, :] = exponents.astype(jnp.int16)
        return carry

    lax.fori_loop(0, out_ref.shape[0], message, 0)


def sum_kernel(parts_ref, out_ref):
    messages, _, lanes = parts_ref.shape
    tiles = out_ref.shape[1] // lanes
    scales = [
        jnp.exp2(parts_ref[d, tiles * ROWS :, :].astype(jnp.int32).astype(jnp.float32) - STEPS) for d in range(messages)
    ]
    for t in range(tiles):
        total = jnp.zeros((ROWS, lanes), jnp.float32)
        for d in range(messages):
            coded = parts_ref[d, t * ROWS : (t + 1) * ROWS, :].astype(jnp.int32)
            total = total + coded.astype(jnp.float32) * scales[d][t : t + 1, :]
        out_ref[:, t * lanes : (t + 1) * lanes] = total


def contract(own, other):
    wide = own[0].shape[-1]
    *early, last = range(len(PARTS))
    depths = [o.shape[0] for o in other]
    gathered = lambda parts: pltpu.VMEM((max(depths[p] for p in parts), wide), jnp.bfloat16)
    cost = lambda parts: pl.CostEstimate(
        flops=2 * sum(depths[p] for p in parts) * wide * HALF,
        bytes_accessed=8 * sum(depths[p] for p in parts) * wide,
        transcendentals=0,
    )
    params = pltpu.CompilerParams(vmem_limit_bytes=32 * 2**20)
    first = pl.pallas_call(
        functools.partial(first_parts_kernel, early),
        out_shape=jax.ShapeDtypeStruct((HALF, wide), jnp.float32),
        in_specs=[VMEM] * (len(PARTS) + len(early)),
        out_specs=VMEM,
        scratch_shapes=[gathered(early)],
        compiler_params=params,
        cost_estimate=cost(early),
    )(*own, *[other[p] for p in early])
    lanes = 128
    return pl.pallas_call(
        functools.partial(last_part_kernel, [last]),
        out_shape=jax.ShapeDtypeStruct((HALF // ROWS, wide // lanes * ROWS + 16, lanes), jnp.int16),
        in_specs=[VMEM] * (len(PARTS) + 2),
        out_specs=VMEM,
        scratch_shapes=[gathered([last]), pltpu.VMEM((HALF, wide), jnp.float32)],
        compiler_params=params,
        cost_estimate=cost([last]),
    )(*own, other[last], first)


def along(first, second, step):
    pairs = []
    for ring in groups(first, second):
        pairs += [(ring[i], ring[(i + (step if i % 2 == 0 else -step)) % N]) for i in range(N)]
    return pairs


def per_device(coefficients, row_weight, pattern, aux_sizes):
    rows = coefficients.shape[0]
    swap = [(0, 1), (1, 0)]
    send, keep = operands(coefficients, row_weight, pattern, aux_sizes)
    blocks = lax.dynamic_update_slice(keep, lax.ppermute(send, "c", swap), (0, rows, 0))
    wide = blocks.shape[2]
    blocks = exchange(blocks, "y", "z").reshape(N, 2, rows, wide)
    move = lambda value, step: lax.ppermute(value, AXES, along("z", "y", step))
    slot = {0: blocks, -2: move(blocks, 2), -1: move(blocks, -1), 1: move(blocks, 1)}
    slot[2] = move(slot[-1], 1)
    slot[4], slot[3], slot[-3] = move(slot[-2], 2), move(slot[-2], 1), move(slot[2], -1)
    own = [jnp.stack([slot[k] for k in OFFSETS[slice(*part)]]) for part in PARTS]
    other = [lax.ppermute(part, "c", swap).reshape(-1, wide) for part in own]
    messages = contract(own, other)
    parts = lax.all_to_all(messages, "x", 0, 0, tiled=True)
    return pl.pallas_call(
        sum_kernel,
        out_shape=jax.ShapeDtypeStruct((ROWS, wide), jnp.float32),
        in_specs=[VMEM],
        out_specs=VMEM,
        compiler_params=SMALL,
    )(parts)


def solution(mesh):
    grid = Mesh(mesh.devices.reshape(N, N, N, 2), AXES)
    placed = (P(AXES, None), P(AXES), P(), P())
    return jax.shard_map(
        per_device,
        mesh=grid,
        in_specs=placed,
        out_specs=P(("y", "x", "c"), "z"),
        check_vma=False,
    )
```

```python
import functools
import itertools

import jax
import jax.numpy as jnp
from jax import lax
from jax.experimental import pallas as pl
from jax.experimental.pallas import tpu as pltpu
from jax.sharding import Mesh, PartitionSpec as P

PAIR_ROWS = 128
AUX_PAD = 128
N = 8
AXES = ("y", "x", "z", "c")
HALF = 384
ROWS = 48
OFFSETS = (0, -2, 2, 1, -1, 4, 3, -3)
PARTS = ((0, 3), (3, 6), (6, 8))
STEPS = 14
VMEM = pl.BlockSpec(memory_space=pltpu.VMEM)
SMALL = pltpu.CompilerParams(vmem_limit_bytes=8 * 2**20)


def groups(first, second):
    found = []
    for core, axis in enumerate((first, second)):
        rest = [a for a in "yxz" if a != axis]
        for others in itertools.product(range(N), repeat=2):
            at = dict(zip(rest, others))
            ring = []
            for i in range(N):
                at[axis] = i
                ring.append(((at["y"] * N + at["x"]) * N + at["z"]) * 2 + core)
            found.append(ring)
    return found


def exchange(blocks, first, second):
    return lax.all_to_all(
        blocks, AXES, 0, 0, tiled=True, axis_index_groups=groups(first, second)
    )


def into_order(tiles):
    lanes = tiles[0].shape[1]
    lane = lax.broadcasted_iota(jnp.int32, tiles[0].shape, 1)
    out = [None] * len(tiles)
    for piece in range(2 * N):
        core, x = divmod(piece, N)
        to, source = piece * ROWS, (2 * x + core) * ROWS
        end = to + ROWS
        while to < end:
            count = min(end - to, lanes - to % lanes, lanes - source % lanes)
            tile, start = divmod(to, lanes)
            rolled = tiles[source // lanes]
            if (to - source) % lanes:
                rolled = pltpu.roll(rolled, (to - source) % lanes, 1)
            out[tile] = rolled if start == 0 else jnp.where(lane >= start, rolled, out[tile])
            to, source = to + count, source + count
    return out


def as_column(row):
    n = row.shape[1]
    square = (n, n)
    here = lax.broadcasted_iota(jnp.int32, square, 0) == lax.broadcasted_iota(jnp.int32, square, 1)
    return jnp.sum(jnp.where(here, jnp.broadcast_to(row, square), 0.0), axis=1, keepdims=True)


def mask_kernel(coef_ref, limits_ref, weight_ref, send_ref, keep_ref):
    rows, width = coef_ref.shape
    tiles = width // N // AUX_PAD
    core = lax.axis_index("c")
    device = ((lax.axis_index("y") * N + lax.axis_index("x")) * N + lax.axis_index("z")) * 2 + core
    block = device * rows // PAIR_ROWS
    lane = lax.broadcasted_iota(jnp.int32, (rows, AUX_PAD), 1)
    at_block = lax.broadcasted_iota(jnp.int32, limits_ref.shape, 1) == block
    limits = jnp.sum(jnp.where(at_block, limits_ref[...], 0), axis=1, keepdims=True)
    limits = jnp.broadcast_to(limits, limits_ref.shape)
    weight = jnp.broadcast_to(as_column(weight_ref[...]), (rows, AUX_PAD))

    def store(ref, to, found):
        for t in range(tiles):
            ref[to, 0:rows, t * AUX_PAD : (t + 1) * AUX_PAD] = found[t].astype(jnp.bfloat16)

    def run(left_ref, right_ref):
        for to in range(N):
            masked = []
            for atom in range(to * tiles, (to + 1) * tiles):
                coef = coef_ref[:, atom * AUX_PAD : (atom + 1) * AUX_PAD].astype(jnp.float32)
                masked.append(jnp.where(lane < limits[atom : atom + 1, :], coef, 0.0))
            store(left_ref, to, into_order(masked))
            store(right_ref, to, [weight * m for m in masked])

    @pl.when(core == 0)
    def _():
        run(keep_ref, send_ref)

    @pl.when(core == 1)
    def _():
        run(send_ref, keep_ref)


def operands(coefficients, row_weight, pattern, aux_sizes):
    rows, width = coefficients.shape
    limits = pattern.T * aux_sizes[:, None]
    return pl.pallas_call(
        mask_kernel,
        out_shape=[jax.ShapeDtypeStruct((N, height, width // N), jnp.bfloat16) for height in (rows, 2 * rows)],
        in_specs=[VMEM] * 3,
        out_specs=[VMEM] * 2,
        compiler_params=SMALL,
        cost_estimate=pl.CostEstimate(flops=8 * rows * width, bytes_accessed=6 * rows * width, transcendentals=0),
    )(coefficients, limits, row_weight.reshape(1, -1))


def away(place, offset):
    return lax.rem(place + (1 - 2 * lax.rem(place, 2)) * offset + N, N)


def contract_part(own_refs, other_ref, gathered, part, write):
    places, two, rows, wide = own_refs[0].shape[1:]
    core = lax.axis_index("c")
    mine = jnp.where(core == 0, lax.axis_index("z"), lax.axis_index("y"))
    theirs = jnp.where(core == 0, lax.axis_index("y"), lax.axis_index("z"))
    tile = 256

    def gather(columns):
        for k, offset in enumerate(OFFSETS[slice(*PARTS[part])]):
            inner = away(theirs, offset)
            for own_ref, (first, last) in zip(own_refs, PARTS):
                for slot in range(first, last):
                    place = away(mine, OFFSETS[slot])
                    for h in range(two):
                        at = pl.multiple_of(((k * places + place) * two + h) * rows, rows)
                        gathered[pl.ds(at, rows), columns] = own_ref[slot - first, inner, 1 - h, :, columns]

    depth = other_ref.shape[0]

    def run(left_ref, right_ref, columns):
        def column_tile(t, carry):
            start = pl.multiple_of(t * tile, tile)
            write(
                start,
                lax.dot_general(
                    left_ref[0:depth, columns],
                    right_ref[0:depth, pl.ds(start, tile)],
                    (((0,), (0,)), ((), ())),
                    preferred_element_type=jnp.float32,
                ),
            )
            return carry

        lax.fori_loop(0, wide // tile, column_tile, 0)

    @pl.when(core == 0)
    def _():
        gather(slice(0, HALF))
        run(gathered, other_ref, slice(0, HALF))

    @pl.when(core == 1)
    def _():
        gather(slice(0, wide))
        run(other_ref, gathered, slice(HALF, 2 * HALF))


def contract_parts(parts, own_refs, other_refs, sum_ref, out_ref, gathered):
    for part, other_ref in zip(parts, other_refs):

        def write(start, value, before=sum_ref):
            columns = pl.ds(start, value.shape[1])
            out_ref[:, columns] = value if before is None else before[:, columns] + value

        contract_part(own_refs, other_ref, gathered, part, write)
        sum_ref = out_ref


def early_part_kernel(parts, *refs):
    *refs, out_ref, gathered = refs
    own, other, before = refs[: len(PARTS)], refs[len(PARTS) :][: len(parts)], refs[len(PARTS) + len(parts) :]
    contract_parts(parts, own, other, before[0] if before else None, out_ref, gathered)


def last_part_kernel(parts, *refs):
    own, other, (first_ref, out_ref, gathered, total) = refs[: len(PARTS)], refs[len(PARTS) : -4], refs[-4:]
    contract_parts(parts, own, other, first_ref, total, gathered)

    lanes = out_ref.shape[2]
    tiles = total.shape[1] // lanes
    tail = out_ref.shape[1] - tiles * ROWS
    at_row = lax.broadcasted_iota(jnp.int32, (tail, lanes), 0)

    def message(d, carry):
        rows = pl.ds(pl.multiple_of(d * ROWS, 16), ROWS)
        exponents = jnp.zeros((tail, lanes), jnp.int32)
        for t in range(tiles):
            value = total[rows, t * lanes : (t + 1) * lanes]
            largest = jnp.max(jnp.abs(value), axis=0, keepdims=True)
            exponent = jnp.floor(jnp.log2(jnp.maximum(largest, 2.0**-110)))
            coded = jnp.floor(value * jnp.exp2(STEPS - exponent) + 0.5)
            coded = jnp.clip(coded, -32767.0, 32767.0).astype(jnp.int32)
            out_ref[d, t * ROWS : (t + 1) * ROWS, :] = coded.astype(jnp.int16)
            exponents = jnp.where(at_row == t, exponent.astype(jnp.int32), exponents)
        out_ref[d, tiles * ROWS :, :] = exponents.astype(jnp.int16)
        return carry

    lax.fori_loop(0, out_ref.shape[0], message, 0)


def sum_kernel(parts_ref, out_ref):
    messages, _, lanes = parts_ref.shape
    tiles = out_ref.shape[1] // lanes
    scales = [
        jnp.exp2(parts_ref[d, tiles * ROWS :, :].astype(jnp.int32).astype(jnp.float32) - STEPS) for d in range(messages)
    ]
    for t in range(tiles):
        total = jnp.zeros((ROWS, lanes), jnp.float32)
        for d in range(messages):
            coded = parts_ref[d, t * ROWS : (t + 1) * ROWS, :].astype(jnp.int32)
            total = total + coded.astype(jnp.float32) * scales[d][t : t + 1, :]
        out_ref[:, t * lanes : (t + 1) * lanes] = total


def contract(own, other):
    wide = own[0].shape[-1]
    *early, last = range(len(PARTS))
    depths = [o.shape[0] for o in other]
    gathered = lambda parts: pltpu.VMEM((max(depths[p] for p in parts), wide), jnp.bfloat16)
    cost = lambda parts: pl.CostEstimate(
        flops=2 * sum(depths[p] for p in parts) * wide * HALF,
        bytes_accessed=8 * sum(depths[p] for p in parts) * wide,
        transcendentals=0,
    )
    params = pltpu.CompilerParams(vmem_limit_bytes=32 * 2**20)
    first = []
    for part in early:
        first = [
            pl.pallas_call(
                functools.partial(early_part_kernel, [part]),
                out_shape=jax.ShapeDtypeStruct((HALF, wide), jnp.float32),
                in_specs=[VMEM] * (len(PARTS) + 1 + len(first)),
                out_specs=VMEM,
                scratch_shapes=[gathered([part])],
                compiler_params=params,
                cost_estimate=cost([part]),
            )(*own, other[part], *first)
        ]
    lanes = 128
    return pl.pallas_call(
        functools.partial(last_part_kernel, [last]),
        out_shape=jax.ShapeDtypeStruct((HALF // ROWS, wide // lanes * ROWS + 16, lanes), jnp.int16),
        in_specs=[VMEM] * (len(PARTS) + 2),
        out_specs=VMEM,
        scratch_shapes=[gathered([last]), pltpu.VMEM((HALF, wide), jnp.float32)],
        compiler_params=params,
        cost_estimate=cost([last]),
    )(*own, other[last], *first)


def along(first, second, step):
    pairs = []
    for ring in groups(first, second):
        pairs += [(ring[i], ring[(i + (step if i % 2 == 0 else -step)) % N]) for i in range(N)]
    return pairs


def per_device(coefficients, row_weight, pattern, aux_sizes):
    rows = coefficients.shape[0]
    swap = [(0, 1), (1, 0)]
    send, keep = operands(coefficients, row_weight, pattern, aux_sizes)
    blocks = lax.dynamic_update_slice(keep, lax.ppermute(send, "c", swap), (0, rows, 0))
    wide = blocks.shape[2]
    blocks = exchange(blocks, "y", "z").reshape(N, 2, rows, wide)
    move = lambda value, step: lax.ppermute(value, AXES, along("z", "y", step))
    slot = {0: blocks, -2: move(blocks, 2), 2: move(blocks, -2), 1: move(blocks, 1), -1: move(blocks, -1)}
    slot[4], slot[3], slot[-3] = move(slot[-2], 2), move(slot[-2], 1), move(slot[2], -1)
    own = [jnp.stack([slot[k] for k in OFFSETS[slice(*part)]]) for part in PARTS]
    other = [lax.ppermute(part, "c", swap).reshape(-1, wide) for part in own]
    messages = contract(own, other)
    parts = lax.all_to_all(messages, "x", 0, 0, tiled=True)
    return pl.pallas_call(
        sum_kernel,
        out_shape=jax.ShapeDtypeStruct((ROWS, wide), jnp.float32),
        in_specs=[VMEM],
        out_specs=VMEM,
        compiler_params=SMALL,
    )(parts)


def solution(mesh):
    grid = Mesh(mesh.devices.reshape(N, N, N, 2), AXES)
    placed = (P(AXES, None), P(AXES), P(), P())
    return jax.shard_map(
        per_device,
        mesh=grid,
        in_specs=placed,
        out_specs=P(("y", "x", "c"), "z"),
        check_vma=False,
    )
```

```python
import functools
import itertools

import jax
import jax.numpy as jnp
from jax import lax
from jax.experimental import pallas as pl
from jax.experimental.pallas import tpu as pltpu
from jax.sharding import Mesh, PartitionSpec as P

PAIR_ROWS = 128
AUX_PAD = 128
N = 8
AXES = ("y", "x", "z", "c")
HALF = 384
ROWS = 48
OFFSETS = (0, -2, 2, 1, -1, 3, -3, 4)
PARTS = ((0, 4), (4, 8))
STEPS = 14
VMEM = pl.BlockSpec(memory_space=pltpu.VMEM)
SMALL = pltpu.CompilerParams(vmem_limit_bytes=8 * 2**20)


def groups(first, second):
    found = []
    for core, axis in enumerate((first, second)):
        rest = [a for a in "yxz" if a != axis]
        for others in itertools.product(range(N), repeat=2):
            at = dict(zip(rest, others))
            ring = []
            for i in range(N):
                at[axis] = i
                ring.append(((at["y"] * N + at["x"]) * N + at["z"]) * 2 + core)
            found.append(ring)
    return found


def exchange(blocks, first, second):
    return lax.all_to_all(
        blocks, AXES, 0, 0, tiled=True, axis_index_groups=groups(first, second)
    )


def into_order(tiles):
    lanes = tiles[0].shape[1]
    lane = lax.broadcasted_iota(jnp.int32, tiles[0].shape, 1)
    out = [None] * len(tiles)
    for piece in range(2 * N):
        core, x = divmod(piece, N)
        to, source = piece * ROWS, (2 * x + core) * ROWS
        end = to + ROWS
        while to < end:
            count = min(end - to, lanes - to % lanes, lanes - source % lanes)
            tile, start = divmod(to, lanes)
            rolled = tiles[source // lanes]
            if (to - source) % lanes:
                rolled = pltpu.roll(rolled, (to - source) % lanes, 1)
            out[tile] = rolled if start == 0 else jnp.where(lane >= start, rolled, out[tile])
            to, source = to + count, source + count
    return out


def as_column(row):
    n = row.shape[1]
    square = (n, n)
    here = lax.broadcasted_iota(jnp.int32, square, 0) == lax.broadcasted_iota(jnp.int32, square, 1)
    return jnp.sum(jnp.where(here, jnp.broadcast_to(row, square), 0.0), axis=1, keepdims=True)


def mask_kernel(coef_ref, limits_ref, weight_ref, send_ref, keep_ref):
    rows, width = coef_ref.shape
    tiles = width // N // AUX_PAD
    core = lax.axis_index("c")
    device = ((lax.axis_index("y") * N + lax.axis_index("x")) * N + lax.axis_index("z")) * 2 + core
    block = device * rows // PAIR_ROWS
    lane = lax.broadcasted_iota(jnp.int32, (rows, AUX_PAD), 1)
    at_block = lax.broadcasted_iota(jnp.int32, limits_ref.shape, 1) == block
    limits = jnp.sum(jnp.where(at_block, limits_ref[...], 0), axis=1, keepdims=True)
    limits = jnp.broadcast_to(limits, limits_ref.shape)
    weight = jnp.broadcast_to(as_column(weight_ref[...]), (rows, AUX_PAD))

    def store(ref, to, found):
        for t in range(tiles):
            ref[to, 0:rows, t * AUX_PAD : (t + 1) * AUX_PAD] = found[t].astype(jnp.bfloat16)

    def run(left_ref, right_ref):
        for to in range(N):
            masked = []
            for atom in range(to * tiles, (to + 1) * tiles):
                coef = coef_ref[:, atom * AUX_PAD : (atom + 1) * AUX_PAD].astype(jnp.float32)
                masked.append(jnp.where(lane < limits[atom : atom + 1, :], coef, 0.0))
            store(left_ref, to, into_order(masked))
            store(right_ref, to, [weight * m for m in masked])

    @pl.when(core == 0)
    def _():
        run(keep_ref, send_ref)

    @pl.when(core == 1)
    def _():
        run(send_ref, keep_ref)


def operands(coefficients, row_weight, pattern, aux_sizes):
    rows, width = coefficients.shape
    limits = pattern.T * aux_sizes[:, None]
    return pl.pallas_call(
        mask_kernel,
        out_shape=[jax.ShapeDtypeStruct((N, height, width // N), jnp.bfloat16) for height in (rows, 2 * rows)],
        in_specs=[VMEM] * 3,
        out_specs=[VMEM] * 2,
        compiler_params=SMALL,
        cost_estimate=pl.CostEstimate(flops=8 * rows * width, bytes_accessed=6 * rows * width, transcendentals=0),
    )(coefficients, limits, row_weight.reshape(1, -1))


def away(place, offset):
    return lax.rem(place + (1 - 2 * lax.rem(place, 2)) * offset + N, N)


def gather_part(own_refs, gathered, part):
    places, two, rows, wide = own_refs[0].shape[1:]
    core = lax.axis_index("c")
    mine = jnp.where(core == 0, lax.axis_index("z"), lax.axis_index("y"))
    theirs = jnp.where(core == 0, lax.axis_index("y"), lax.axis_index("z"))

    def gather(columns):
        for k, offset in enumerate(OFFSETS[slice(*PARTS[part])]):
            inner = away(theirs, offset)
            for own_ref, (first, last) in zip(own_refs, PARTS):
                for slot in range(first, last):
                    place = away(mine, OFFSETS[slot])
                    for h in range(two):
                        at = pl.multiple_of(((k * places + place) * two + h) * rows, rows)
                        gathered[pl.ds(at, rows), columns] = own_ref[slot - first, inner, 1 - h, :, columns]

    @pl.when(core == 0)
    def _():
        gather(slice(0, HALF))

    @pl.when(core == 1)
    def _():
        gather(slice(0, wide))


def contract_part(gathered, other_ref, write):
    depth, wide = other_ref.shape
    core = lax.axis_index("c")
    tile = 256

    def run(left_ref, right_ref, columns):
        def column_tile(t, carry):
            start = pl.multiple_of(t * tile, tile)
            write(
                start,
                lax.dot_general(
                    left_ref[0:depth, columns],
                    right_ref[0:depth, pl.ds(start, tile)],
                    (((0,), (0,)), ((), ())),
                    preferred_element_type=jnp.float32,
                ),
            )
            return carry

        lax.fori_loop(0, wide // tile, column_tile, 0)

    @pl.when(core == 0)
    def _():
        run(gathered, other_ref, slice(0, HALF))

    @pl.when(core == 1)
    def _():
        run(other_ref, gathered, slice(HALF, 2 * HALF))


def first_part_kernel(own_0, own_1, other_ref, out_ref, ready_ref, gathered):
    def write(start, value):
        out_ref[:, pl.ds(start, value.shape[1])] = value

    own_refs = (own_0, own_1)
    gather_part(own_refs, gathered, 0)
    contract_part(gathered, other_ref, write)
    gather_part(own_refs, ready_ref, 1)


def last_part_kernel(ready_ref, other_ref, first_ref, out_ref, total):
    def write(start, value):
        columns = pl.ds(start, value.shape[1])
        total[:, columns] = first_ref[:, columns] + value

    contract_part(ready_ref, other_ref, write)

    lanes = out_ref.shape[2]
    tiles = total.shape[1] // lanes
    tail = out_ref.shape[1] - tiles * ROWS
    at_row = lax.broadcasted_iota(jnp.int32, (tail, lanes), 0)

    def message(d, carry):
        rows = pl.ds(pl.multiple_of(d * ROWS, 16), ROWS)
        exponents = jnp.zeros((tail, lanes), jnp.int32)
        for t in range(tiles):
            value = total[rows, t * lanes : (t + 1) * lanes]
            largest = jnp.max(jnp.abs(value), axis=0, keepdims=True)
            exponent = jnp.floor(jnp.log2(jnp.maximum(largest, 2.0**-110)))
            coded = jnp.floor(value * jnp.exp2(STEPS - exponent) + 0.5)
            coded = jnp.clip(coded, -32767.0, 32767.0).astype(jnp.int32)
            out_ref[d, t * ROWS : (t + 1) * ROWS, :] = coded.astype(jnp.int16)
            exponents = jnp.where(at_row == t, exponent.astype(jnp.int32), exponents)
        out_ref[d, tiles * ROWS :, :] = exponents.astype(jnp.int16)
        return carry

    lax.fori_loop(0, out_ref.shape[0], message, 0)


def sum_kernel(parts_ref, out_ref):
    messages, _, lanes = parts_ref.shape
    tiles = out_ref.shape[1] // lanes
    scales = [
        jnp.exp2(parts_ref[d, tiles * ROWS :, :].astype(jnp.int32).astype(jnp.float32) - STEPS) for d in range(messages)
    ]
    for t in range(tiles):
        total = jnp.zeros((ROWS, lanes), jnp.float32)
        for d in range(messages):
            coded = parts_ref[d, t * ROWS : (t + 1) * ROWS, :].astype(jnp.int32)
            total = total + coded.astype(jnp.float32) * scales[d][t : t + 1, :]
        out_ref[:, t * lanes : (t + 1) * lanes] = total


def contract(own, other):
    depth, wide = other[0].shape
    cost = pl.CostEstimate(flops=2 * depth * wide * HALF, bytes_accessed=8 * depth * wide, transcendentals=0)
    params = pltpu.CompilerParams(vmem_limit_bytes=32 * 2**20)
    first, ready = pl.pallas_call(
        first_part_kernel,
        out_shape=[
            jax.ShapeDtypeStruct((HALF, wide), jnp.float32),
            jax.ShapeDtypeStruct(other[1].shape, jnp.bfloat16),
        ],
        in_specs=[VMEM] * 3,
        out_specs=[VMEM] * 2,
        scratch_shapes=[pltpu.VMEM((depth, wide), jnp.bfloat16)],
        compiler_params=params,
        cost_estimate=cost,
    )(*own, other[0])
    lanes = 128
    return pl.pallas_call(
        last_part_kernel,
        out_shape=jax.ShapeDtypeStruct((HALF // ROWS, wide // lanes * ROWS + 16, lanes), jnp.int16),
        in_specs=[VMEM] * 3,
        out_specs=VMEM,
        scratch_shapes=[pltpu.VMEM((HALF, wide), jnp.float32)],
        compiler_params=params,
        cost_estimate=cost,
    )(ready, other[1], first)


def along(first, second, step):
    pairs = []
    for ring in groups(first, second):
        pairs += [(ring[i], ring[(i + (step if i % 2 == 0 else -step)) % N]) for i in range(N)]
    return pairs


def per_device(coefficients, row_weight, pattern, aux_sizes):
    rows = coefficients.shape[0]
    swap = [(0, 1), (1, 0)]
    send, keep = operands(coefficients, row_weight, pattern, aux_sizes)
    blocks = lax.dynamic_update_slice(keep, lax.ppermute(send, "c", swap), (0, rows, 0))
    wide = blocks.shape[2]
    blocks = exchange(blocks, "y", "z").reshape(N, 2, rows, wide)
    move = lambda value, step: lax.ppermute(value, AXES, along("z", "y", step))
    slot = {0: blocks, -2: move(blocks, 2), 2: move(blocks, -2), 1: move(blocks, 1), -1: move(blocks, -1)}
    slot[4], slot[3], slot[-3] = move(slot[-2], 2), move(slot[-2], 1), move(slot[2], -1)
    own = [jnp.stack([slot[k] for k in OFFSETS[slice(*part)]]) for part in PARTS]
    other = [lax.ppermute(part, "c", swap).reshape(-1, wide) for part in own]
    messages = contract(own, other)
    parts = lax.all_to_all(messages, "x", 0, 0, tiled=True)
    return pl.pallas_call(
        sum_kernel,
        out_shape=jax.ShapeDtypeStruct((ROWS, wide), jnp.float32),
        in_specs=[VMEM],
        out_specs=VMEM,
        compiler_params=SMALL,
    )(parts)


def solution(mesh):
    grid = Mesh(mesh.devices.reshape(N, N, N, 2), AXES)
    placed = (P(AXES, None), P(AXES), P(), P())
    return jax.shard_map(
        per_device,
        mesh=grid,
        in_specs=placed,
        out_specs=P(("y", "x", "c"), "z"),
        check_vma=False,
    )
```

```python
import functools
import itertools

import jax
import jax.numpy as jnp
from jax import lax
from jax.experimental import pallas as pl
from jax.experimental.pallas import tpu as pltpu
from jax.sharding import Mesh, PartitionSpec as P

PAIR_ROWS = 128
AUX_PAD = 128
N = 8
AXES = ("y", "x", "z", "c")
HALF = 384
ROWS = 48
OFFSETS = (0, -2, 2, 1, -1, 3, -3, 4)
PARTS = ((0, 4), (4, 8))
STEPS = 14
VMEM = pl.BlockSpec(memory_space=pltpu.VMEM)
SMALL = pltpu.CompilerParams(vmem_limit_bytes=8 * 2**20)


def groups(first, second):
    found = []
    for core, axis in enumerate((first, second)):
        rest = [a for a in "yxz" if a != axis]
        for others in itertools.product(range(N), repeat=2):
            at = dict(zip(rest, others))
            ring = []
            for i in range(N):
                at[axis] = i
                ring.append(((at["y"] * N + at["x"]) * N + at["z"]) * 2 + core)
            found.append(ring)
    return found


def exchange(blocks, first, second):
    return lax.all_to_all(
        blocks, AXES, 0, 0, tiled=True, axis_index_groups=groups(first, second)
    )


def into_order(tiles):
    lanes = tiles[0].shape[1]
    lane = lax.broadcasted_iota(jnp.int32, tiles[0].shape, 1)
    out = [None] * len(tiles)
    for piece in range(2 * N):
        core, x = divmod(piece, N)
        to, source = piece * ROWS, (2 * x + core) * ROWS
        end = to + ROWS
        while to < end:
            count = min(end - to, lanes - to % lanes, lanes - source % lanes)
            tile, start = divmod(to, lanes)
            rolled = tiles[source // lanes]
            if (to - source) % lanes:
                rolled = pltpu.roll(rolled, (to - source) % lanes, 1)
            out[tile] = rolled if start == 0 else jnp.where(lane >= start, rolled, out[tile])
            to, source = to + count, source + count
    return out


def as_column(row):
    n = row.shape[1]
    square = (n, n)
    here = lax.broadcasted_iota(jnp.int32, square, 0) == lax.broadcasted_iota(jnp.int32, square, 1)
    return jnp.sum(jnp.where(here, jnp.broadcast_to(row, square), 0.0), axis=1, keepdims=True)


def mask_kernel(coef_ref, limits_ref, weight_ref, send_ref, keep_ref):
    rows, width = coef_ref.shape
    tiles = width // N // AUX_PAD
    core = lax.axis_index("c")
    device = ((lax.axis_index("y") * N + lax.axis_index("x")) * N + lax.axis_index("z")) * 2 + core
    block = device * rows // PAIR_ROWS
    lane = lax.broadcasted_iota(jnp.int32, (rows, AUX_PAD), 1)
    at_block = lax.broadcasted_iota(jnp.int32, limits_ref.shape, 1) == block
    limits = jnp.sum(jnp.where(at_block, limits_ref[...], 0), axis=1, keepdims=True)
    limits = jnp.broadcast_to(limits, limits_ref.shape)
    weight = jnp.broadcast_to(as_column(weight_ref[...]), (rows, AUX_PAD))

    def store(ref, to, found):
        for t in range(tiles):
            ref[to, 0:rows, t * AUX_PAD : (t + 1) * AUX_PAD] = found[t].astype(jnp.bfloat16)

    def run(left_ref, right_ref):
        for to in range(N):
            masked = []
            for atom in range(to * tiles, (to + 1) * tiles):
                coef = coef_ref[:, atom * AUX_PAD : (atom + 1) * AUX_PAD].astype(jnp.float32)
                masked.append(jnp.where(lane < limits[atom : atom + 1, :], coef, 0.0))
            store(left_ref, to, into_order(masked))
            store(right_ref, to, [weight * m for m in masked])

    @pl.when(core == 0)
    def _():
        run(keep_ref, send_ref)

    @pl.when(core == 1)
    def _():
        run(send_ref, keep_ref)


def operands(coefficients, row_weight, pattern, aux_sizes):
    rows, width = coefficients.shape
    limits = pattern.T * aux_sizes[:, None]
    return pl.pallas_call(
        mask_kernel,
        out_shape=[jax.ShapeDtypeStruct((N, height, width // N), jnp.bfloat16) for height in (rows, 2 * rows)],
        in_specs=[VMEM] * 3,
        out_specs=[VMEM] * 2,
        compiler_params=SMALL,
        cost_estimate=pl.CostEstimate(flops=8 * rows * width, bytes_accessed=6 * rows * width, transcendentals=0),
    )(coefficients, limits, row_weight.reshape(1, -1))


def away(place, offset):
    return lax.rem(place + (1 - 2 * lax.rem(place, 2)) * offset + N, N)


def contract_part(own_refs, other_ref, gathered, part, write):
    places, two, rows, wide = own_refs[0].shape[1:]
    core = lax.axis_index("c")
    mine = jnp.where(core == 0, lax.axis_index("z"), lax.axis_index("y"))
    theirs = jnp.where(core == 0, lax.axis_index("y"), lax.axis_index("z"))
    tile = 256

    def gather(columns):
        for k, offset in enumerate(OFFSETS[slice(*PARTS[part])]):
            inner = away(theirs, offset)
            for own_ref, (first, last) in zip(own_refs, PARTS):
                for slot in range(first, last):
                    place = away(mine, OFFSETS[slot])
                    for h in range(two):
                        at = pl.multiple_of(((k * places + place) * two + h) * rows, rows)
                        gathered[pl.ds(at, rows), columns] = own_ref[slot - first, inner, 1 - h, :, columns]

    depth = other_ref.shape[0]

    def run(left_ref, right_ref, columns):
        def column_tile(t, carry):
            start = pl.multiple_of(t * tile, tile)
            write(
                start,
                lax.dot_general(
                    left_ref[0:depth, columns],
                    right_ref[0:depth, pl.ds(start, tile)],
                    (((0,), (0,)), ((), ())),
                    preferred_element_type=jnp.float32,
                ),
            )
            return carry

        lax.fori_loop(0, wide // tile, column_tile, 0)

    @pl.when(core == 0)
    def _():
        gather(slice(0, HALF))
        run(gathered, other_ref, slice(0, HALF))

    @pl.when(core == 1)
    def _():
        gather(slice(0, wide))
        run(other_ref, gathered, slice(HALF, 2 * HALF))


def contract_parts(parts, own_refs, other_refs, sum_ref, out_ref, gathered):
    for part, other_ref in zip(parts, other_refs):

        def write(start, value, before=sum_ref):
            columns = pl.ds(start, value.shape[1])
            out_ref[:, columns] = value if before is None else before[:, columns] + value

        contract_part(own_refs, other_ref, gathered, part, write)
        sum_ref = out_ref


def first_parts_kernel(parts, *refs):
    own, other, (out_ref, gathered) = refs[: len(PARTS)], refs[len(PARTS) : -2], refs[-2:]
    contract_parts(parts, own, other, None, out_ref, gathered)


def last_part_kernel(parts, *refs):
    own, other, (first_ref, out_ref, gathered, total) = refs[: len(PARTS)], refs[len(PARTS) : -4], refs[-4:]
    contract_parts(parts, own, other, first_ref, total, gathered)

    lanes = out_ref.shape[2]
    tiles = total.shape[1] // lanes
    tail = out_ref.shape[1] - tiles * ROWS
    at_row = lax.broadcasted_iota(jnp.int32, (tail, lanes), 0)

    def message(d, carry):
        rows = pl.ds(pl.multiple_of(d * ROWS, 16), ROWS)
        exponents = jnp.zeros((tail, lanes), jnp.int32)
        for t in range(tiles):
            value = total[rows, t * lanes : (t + 1) * lanes]
            largest = jnp.max(jnp.abs(value), axis=0, keepdims=True)
            exponent = jnp.floor(jnp.log2(jnp.maximum(largest, 2.0**-110)))
            coded = jnp.floor(value * jnp.exp2(STEPS - exponent) + 0.5)
            coded = jnp.clip(coded, -32767.0, 32767.0).astype(jnp.int32)
            out_ref[d, t * ROWS : (t + 1) * ROWS, :] = coded.astype(jnp.int16)
            exponents = jnp.where(at_row == t, exponent.astype(jnp.int32), exponents)
        out_ref[d, tiles * ROWS :, :] = exponents.astype(jnp.int16)
        return carry

    lax.fori_loop(0, out_ref.shape[0], message, 0, unroll=True)


def sum_kernel(parts_ref, out_ref):
    messages, _, lanes = parts_ref.shape
    tiles = out_ref.shape[1] // lanes
    scales = [
        jnp.exp2(parts_ref[d, tiles * ROWS :, :].astype(jnp.int32).astype(jnp.float32) - STEPS) for d in range(messages)
    ]
    for t in range(tiles):
        total = jnp.zeros((ROWS, lanes), jnp.float32)
        for d in range(messages):
            coded = parts_ref[d, t * ROWS : (t + 1) * ROWS, :].astype(jnp.int32)
            total = total + coded.astype(jnp.float32) * scales[d][t : t + 1, :]
        out_ref[:, t * lanes : (t + 1) * lanes] = total


def contract(own, other):
    wide = own[0].shape[-1]
    *early, last = range(len(PARTS))
    depths = [o.shape[0] for o in other]
    gathered = lambda parts: pltpu.VMEM((max(depths[p] for p in parts), wide), jnp.bfloat16)
    cost = lambda parts: pl.CostEstimate(
        flops=2 * sum(depths[p] for p in parts) * wide * HALF,
        bytes_accessed=8 * sum(depths[p] for p in parts) * wide,
        transcendentals=0,
    )
    params = pltpu.CompilerParams(vmem_limit_bytes=32 * 2**20)
    first = pl.pallas_call(
        functools.partial(first_parts_kernel, early),
        out_shape=jax.ShapeDtypeStruct((HALF, wide), jnp.float32),
        in_specs=[VMEM] * (len(PARTS) + len(early)),
        out_specs=VMEM,
        scratch_shapes=[gathered(early)],
        compiler_params=params,
        cost_estimate=cost(early),
    )(*own, *[other[p] for p in early])
    lanes = 128
    return pl.pallas_call(
        functools.partial(last_part_kernel, [last]),
        out_shape=jax.ShapeDtypeStruct((HALF // ROWS, wide // lanes * ROWS + 16, lanes), jnp.int16),
        in_specs=[VMEM] * (len(PARTS) + 2),
        out_specs=VMEM,
        scratch_shapes=[gathered([last]), pltpu.VMEM((HALF, wide), jnp.float32)],
        compiler_params=params,
        cost_estimate=cost([last]),
    )(*own, other[last], first)


def along(first, second, step):
    pairs = []
    for ring in groups(first, second):
        pairs += [(ring[i], ring[(i + (step if i % 2 == 0 else -step)) % N]) for i in range(N)]
    return pairs


def per_device(coefficients, row_weight, pattern, aux_sizes):
    rows = coefficients.shape[0]
    swap = [(0, 1), (1, 0)]
    send, keep = operands(coefficients, row_weight, pattern, aux_sizes)
    blocks = lax.dynamic_update_slice(keep, lax.ppermute(send, "c", swap), (0, rows, 0))
    wide = blocks.shape[2]
    blocks = exchange(blocks, "y", "z").reshape(N, 2, rows, wide)
    move = lambda value, step: lax.ppermute(value, AXES, along("z", "y", step))
    slot = {0: blocks, -2: move(blocks, 2), 2: move(blocks, -2), 1: move(blocks, 1), -1: move(blocks, -1)}
    slot[4], slot[3], slot[-3] = move(slot[-2], 2), move(slot[-2], 1), move(slot[2], -1)
    own = [jnp.stack([slot[k] for k in OFFSETS[slice(*part)]]) for part in PARTS]
    other = [lax.ppermute(part, "c", swap).reshape(-1, wide) for part in own]
    messages = contract(own, other)
    parts = lax.all_to_all(messages, "x", 0, 0, tiled=True)
    return pl.pallas_call(
        sum_kernel,
        out_shape=jax.ShapeDtypeStruct((ROWS, wide), jnp.float32),
        in_specs=[VMEM],
        out_specs=VMEM,
        compiler_params=SMALL,
    )(parts)


def solution(mesh):
    grid = Mesh(mesh.devices.reshape(N, N, N, 2), AXES)
    placed = (P(AXES, None), P(AXES), P(), P())
    return jax.shard_map(
        per_device,
        mesh=grid,
        in_specs=placed,
        out_specs=P(("y", "x", "c"), "z"),
        check_vma=False,
    )
```
